32 devices in a mesh: inner: 8 (over y, x, core), outer: 4 (over z).
Axes of the slice: x: 2, y: 2, z: 4, core: 2. Of those that a mesh axis runs over, the one named last changes fastest.
Arguments:
- gradients: bfloat16 [8, 4, 256, 8192], P('inner', 'outer'), may hold values from -6 to 6
- master_shard: float32 [256, 8192], P('outer', 'inner'), may hold values from -6 to 6
- first_moment: float32 [256, 8192], P('outer', 'inner'), may hold values from -48 to 48
- second_moment: float32 [256, 8192], P('outer', 'inner'), may hold values from 100 to 1000
Outputs:
- new_master: float32 [256, 8192], P('outer', 'inner')
- new_first: float32 [256, 8192], P('outer', 'inner')
- new_second: float32 [256, 8192], P('outer', 'inner')
- group_weights: bfloat16 [256, 8192], P(None, 'inner')
The draws below stay inside these ranges and needn't reach their ends.
All inputs are finite; a program needn't handle non-finite values.
Results may differ from the reference program's by a relative error of at most 0.0025.
Values may be sent and summed in bfloat16 or wider, within the bound.
No kernel may reach another device: no remote copies, remote signals or barrier semaphores. Data moves between devices by JAX's collectives and lax.ppermute only.
A program may use at most 64 MiB of HBM per device.

```python
import math
import jax
import jax.numpy as jnp
from jax import lax

D = 8192
ROWS = 256
N_INNER = 8
N_OUTER = 4


def spiked(result, stream_key, source, target, shards_of, factor):
    owner, partner = [(jnp.arange(result.shape[position]) // (result.shape[position] // shards_of)).reshape([-1 if axis == position else 1 for axis in range(result.ndim)]) for position in (source, target)]
    chosen = jax.random.permutation(stream_key, shards_of)[partner]
    strong = (owner == chosen) | (owner == (partner + shards_of // 2) % shards_of)
    return jnp.where(strong, factor * result, result)


def steps_of(rng, dims, shards, least, high):
    level = 1.0
    for axis_at, parts in shards:
        heights = jax.random.uniform(jax.random.fold_in(jax.random.fold_in(rng, 6), axis_at), (parts,), jnp.float32, least / len(shards), high / len(shards))
        level = level * jnp.repeat(jnp.exp(heights), dims[axis_at] // parts).reshape((-1,) + (1,) * (len(dims) - 1 - axis_at))
    return level


def centred(stream_key, extent, spread, bound, cuts=(), dtype=jnp.bfloat16):
    drawn = spread * jax.random.normal(stream_key, extent, jnp.float32)
    if cuts:
        drawn = drawn * steps_of(stream_key, extent, cuts, -0.22, 0.18)
    return jnp.clip(drawn, -bound, bound).astype(dtype)


def noise_with(stream_key, extent, width, bound, shards, heavy, held_as=jnp.bfloat16):
    values = width * jax.random.normal(stream_key, extent, jnp.float32)
    if shards:
        values = values * steps_of(stream_key, extent, shards, -0.22, 0.18)
    return jnp.clip(spiked(values, jax.random.fold_in(stream_key, 3), *heavy), -bound, bound).astype(held_as)


def setup_inputs(seed: int = 0) -> dict:
    arg_keys = jax.random.split(jax.random.key(seed), 5)
    gradients = noise_with(arg_keys[0], (N_INNER, N_OUTER, ROWS, D), 1.0, 6.0, ((0, 8), (1, 4)), (1, 2, 4, 2.0))
    master_shard = centred(arg_keys[1], (ROWS, D), 1.0, 6.0, ((0, 4), (1, 8)), jnp.float32)
    first_moment = centred(arg_keys[2], (ROWS, D), 8.0, 48.0, ((0, 4), (1, 8)), jnp.float32)
    second_moment = jnp.clip(jnp.exp(math.log(1000.0) - 2.3025851 * jax.random.uniform(arg_keys[3], (ROWS, D), jnp.float32) ** steps_of(arg_keys[3], (ROWS, D), ((0, 4), (1, 8)), -0.2, 0.2)), 100.0, 1000.0)
    return dict(gradients=gradients, master_shard=master_shard, first_moment=first_moment, second_moment=second_moment)


beta_first = 0.9
beta_second = 0.95
learn_rate = 0.05
decay_rate = 0.1
adam_eps = 1e-05
bias_first = 1.0 - 0.9 ** 10
bias_second = 1.0 - 0.95 ** 10

def reference(gradients, master_shard, first_moment, second_moment):
    total = lax.optimization_barrier(jnp.sum(gradients.astype(jnp.float32), axis=(0, 1)))
    new_first = beta_first * first_moment + (1.0 - beta_first) * total
    new_second = beta_second * second_moment + (1.0 - beta_second) * total * total
    update = new_first / bias_first / (jnp.sqrt(new_second / bias_second) + adam_eps) + decay_rate * master_shard
    new_master = master_shard - learn_rate * update
    group_weights = new_master.astype(jnp.bfloat16)
    return (new_master, new_first, new_second, group_weights)
```

```python
import functools

import jax
import jax.numpy as jnp
from jax import lax
from jax.experimental import pallas as pl
from jax.experimental.pallas import tpu as pltpu
from jax.sharding import PartitionSpec as P

beta_first = 0.9
beta_second = 0.95
learn_rate = 0.05
decay_rate = 0.1
adam_eps = 1e-05
bias_first = 1.0 - 0.9**10
bias_second = 1.0 - 0.95**10

CORES = 2
SUPERS = 2
STEP = 16
ANY = pl.BlockSpec(memory_space=pl.ANY)
VMEM = pl.BlockSpec(memory_space=pltpu.VMEM)


def estimate(nbytes):
    return pl.CostEstimate(flops=nbytes, bytes_accessed=nbytes, transcendentals=0)


def place(chips):
    me = lax.axis_index("inner")
    return me // CORES, lax.rem(me, CORES)


def grad_block(grad_ref, rows, chip, core, width):
    start = pl.multiple_of((CORES * chip + core) * width, width)
    return grad_ref.at[:, pl.ds(*rows), pl.ds(start, width)]


def load(sources, slots, sems):
    copies = [pltpu.make_async_copy(s, d, sems.at[i]) for i, (s, d) in enumerate(zip(sources, slots))]
    for copy in copies:
        copy.start()
    for copy in copies:
        copy.wait()


def total_of(terms, index):
    value = terms[0][index].astype(jnp.float32)
    for term in terms[1:]:
        value = value + term[index].astype(jnp.float32)
    return value


def add_pieces(out, terms):
    blocks, depth, _ = terms[0].shape
    per = depth // STEP

    def step(i, carry):
        index = (i // per, pl.ds(pl.multiple_of(lax.rem(i, per) * STEP, STEP), STEP))
        out[index] = total_of(terms, index).astype(out.dtype)
        return carry

    lax.fori_loop(0, blocks * per, step, 0)


def pack(grads, rows, width, chips):
    outer = grads.shape[0]

    def kernel(grad_ref, out_ref, sems):
        _, core = place(chips)
        load(
            [grad_block(grad_ref, rows, chip, 1 - core, width) for chip in range(chips)],
            [out_ref.at[chip] for chip in range(chips)],
            sems,
        )

    shape = (chips, outer, rows[1], width)
    return pl.pallas_call(
        kernel,
        out_shape=jax.ShapeDtypeStruct(shape, grads.dtype),
        in_specs=[ANY],
        out_specs=ANY,
        scratch_shapes=[pltpu.SemaphoreType.DMA((chips,))],
        cost_estimate=estimate(2 * 2 * chips * outer * rows[1] * width),
        name="pack",
    )(grads)


def sums(grads, core_in, extra, rows, width, chips, targets, name):
    outer = grads.shape[0]
    n_terms = [2 + len(t["extra"]) for t in targets]
    total = sum(n_terms)

    def kernel(*refs):
        grad_ref, core_ref = refs[:2]
        extra_refs = refs[2 : 2 + len(extra)]
        outs = refs[2 + len(extra) : 2 + len(extra) + len(targets)]
        slots = refs[2 + len(extra) + len(targets) : -1]
        sems = refs[-1]
        chip, core = place(chips)
        groups, at = [], 0
        for t, n in zip(targets, n_terms):
            to = t["chip"](chip)
            base, depth = t["rows"]
            sources = [
                grad_block(grad_ref, (rows[0] + base, depth), to, core, width),
                core_ref.at[to, :, pl.ds(base, depth)],
            ] + [extra_refs[i].at[j] if j is not None else extra_refs[i] for i, j in t["extra"]]
            copies = [
                pltpu.make_async_copy(s, slots[at + i], sems.at[at + i]) for i, s in enumerate(sources)
            ]
            for copy in copies:
                copy.start()
            groups.append((copies, slots[at : at + n]))
            at += n
        for (copies, terms), out in zip(groups, outs):
            for copy in copies:
                copy.wait()
            add_pieces(out, terms)

    shapes = [(outer, t["rows"][1], width) for t in targets]
    scratch = [pltpu.VMEM(s, jnp.bfloat16) for s, n in zip(shapes, n_terms) for _ in range(n)]
    return pl.pallas_call(
        kernel,
        out_shape=[jax.ShapeDtypeStruct(s, jnp.bfloat16) for s in shapes],
        in_specs=[ANY] * (2 + len(extra)),
        out_specs=[VMEM] * len(targets),
        scratch_shapes=scratch + [pltpu.SemaphoreType.DMA((total,))],
        cost_estimate=estimate(sum(2 * (n + 1) * s[0] * s[1] * s[2] for s, n in zip(shapes, n_terms))),
        name=name,
    )(grads, core_in, *extra)


def group_sum(grads, core_in, extra, rows, width, chips, parts):
    outer = grads.shape[0]
    depth = rows[1]
    n_terms = [2 + len(p["extra"]) for p in parts]
    total = sum(n_terms)

    def kernel(*refs):
        grad_ref, core_ref = refs[:2]
        extra_refs = refs[2 : 2 + len(extra)]
        outs = refs[2 + len(extra) : 2 + len(extra) + outer]
        slots = refs[2 + len(extra) + outer : -1]
        sems = refs[-1]
        chip, core = place(chips)
        here = lax.axis_index("outer")
        groups, at = [], 0
        for p, n in zip(parts, n_terms):
            base, size = p["rows"]
            sources = [
                grad_block(grad_ref, (rows[0] + base, size), chip, core, width),
                core_ref.at[chip, :, pl.ds(base, size)],
            ] + [extra_refs[i].at[j] if j is not None else extra_refs[i] for i, j in p["extra"]]
            copies = [
                pltpu.make_async_copy(s, slots[at + i], sems.at[at + i]) for i, s in enumerate(sources)
            ]
            for copy in copies:
                copy.start()
            groups.append((copies, slots[at : at + n], base, size))
            at += n
        for copies, terms, base, size in groups:
            for copy in copies:
                copy.wait()
            for shift in range(outer):
                block = lax.rem(here + shift, outer)
                for at in range(0, size, STEP):
                    value = total_of(terms, (block, pl.ds(at, STEP)))
                    outs[shift][pl.ds(base + at, STEP)] = value.astype(outs[shift].dtype)

    shapes = [(outer, p["rows"][1], width) for p in parts]
    scratch = [pltpu.VMEM(s, jnp.bfloat16) for s, n in zip(shapes, n_terms) for _ in range(n)]
    return pl.pallas_call(
        kernel,
        out_shape=[
            jax.ShapeDtypeStruct((depth, width), jnp.float32 if s == 0 else jnp.bfloat16) for s in range(outer)
        ],
        in_specs=[ANY] * (2 + len(extra)),
        out_specs=[VMEM] * outer,
        scratch_shapes=scratch + [pltpu.SemaphoreType.DMA((total,))],
        cost_estimate=estimate(sum(2 * (n + 1) * s[0] * s[1] * s[2] for s, n in zip(shapes, n_terms))),
        name="group_sum",
    )(grads, core_in, *extra)


def adam(total, master, first, second):
    new_first = beta_first * first + (1.0 - beta_first) * total
    new_second = beta_second * second + (1.0 - beta_second) * total * total
    update = new_first / bias_first / (jnp.sqrt(new_second / bias_second) + adam_eps) + decay_rate * master
    return master - learn_rate * update, new_first, new_second


def weights(kept, received, rows, master, first, second):
    depth, width = kept.shape

    def kernel(*refs):
        *terms, master_ref, first_ref, second_ref, out_ref = refs

        def step(i, carry):
            here = pl.ds(pl.multiple_of(i * STEP, STEP), STEP)
            there = pl.ds(pl.multiple_of(rows[0] + i * STEP, STEP), STEP)
            value, _, _ = adam(total_of(terms, here), master_ref[there], first_ref[there], second_ref[there])
            out_ref[here] = value.astype(jnp.bfloat16)
            return carry

        lax.fori_loop(0, depth // STEP, step, 0)

    return pl.pallas_call(
        kernel,
        out_shape=jax.ShapeDtypeStruct((depth, width), jnp.bfloat16),
        in_specs=[VMEM] * (4 + len(received)),
        out_specs=VMEM,
        cost_estimate=estimate(depth * width * 24),
        name="weights",
    )(kept, *received, master, first, second)


def finish(totals, spans, master, first, second):
    n = len(totals[0])

    def kernel(*refs):
        terms = refs[: n * len(spans)]
        master_ref, first_ref, second_ref, *outs = refs[n * len(spans) :]
        for k, (base, depth) in enumerate(spans):

            def step(i, carry, k=k, base=base):
                here = pl.ds(pl.multiple_of(i * STEP, STEP), STEP)
                there = pl.ds(pl.multiple_of(base + i * STEP, STEP), STEP)
                values = adam(
                    total_of(terms[n * k : n * k + n], here), master_ref[there], first_ref[there], second_ref[there]
                )
                for out, value in zip(outs, values):
                    out[there] = value
                return carry

            lax.fori_loop(0, depth // STEP, step, 0)

    return pl.pallas_call(
        kernel,
        out_shape=[jax.ShapeDtypeStruct(master.shape, jnp.float32)] * 3,
        in_specs=[VMEM] * (n * len(spans) + 3),
        out_specs=[VMEM] * 3,
        cost_estimate=estimate(master.size * 34),
        name="finish",
    )(*[t for group in totals for t in group], master, first, second)


def assemble(own, received, spans, outer, owned):
    width = own[0].shape[1]

    def kernel(*refs):
        *pieces, out_ref, sems = refs
        here = lax.axis_index("outer")
        sources, places = [], []
        at = 0
        for base, depth in spans:
            for shift in range(outer):
                block = lax.rem(here + outer - shift, outer)
                sources.append(pieces[at])
                places.append(out_ref.at[block, pl.ds(base, depth)])
                at += 1
        load(sources, places, sems)

    return pl.pallas_call(
        kernel,
        out_shape=jax.ShapeDtypeStruct((outer, owned, width), jnp.bfloat16),
        in_specs=[ANY] * (outer * len(spans)),
        out_specs=ANY,
        scratch_shapes=[pltpu.SemaphoreType.DMA((outer * len(spans),))],
        cost_estimate=estimate(4 * outer * owned * width),
        name="assemble",
    )(*[piece for w, got in zip(own, received) for piece in (w, *got)])


def to_chip(x, target, chips):
    pairs = [(CORES * c + k, CORES * target(c) + k) for c in range(chips) for k in range(CORES)]
    return lax.ppermute(x, "inner", pairs)


def to_group(x, shift, outer):
    return lax.ppermute(x, "outer", [(i, (i + shift) % outer) for i in range(outer)])


def body(gradients, master, first, second, *, inner, outer):
    depth, columns = gradients.shape[2:]
    chips, owned, width = inner // CORES, depth // outer, columns // inner
    grads = gradients.reshape(outer, owned, columns)

    supers = SUPERS if owned % (2 * STEP * SUPERS) == 0 else 1
    per = owned // supers
    spans = [(k * per, per) for k in range(supers)]
    two_steps = chips == 4 and per % (2 * STEP) == 0

    totals, own, received = [], [], []
    for rows in spans:
        packed = pack(grads, rows, width, chips)
        core_in = lax.ppermute(packed, "inner", [(i, i ^ 1) for i in range(inner)])
        if two_steps:
            half = per // 2
            runs = [((0, half), 1, 2), ((half, half), 2, 1)]
            targets = [
                dict(rows=run, chip=lambda c, t=t: c ^ t, extra=[])
                for run, a, b in runs
                for t in (a, a ^ b)
            ]
            made = sums(grads, core_in, [], rows, width, chips, targets, "first_sum")
            got = [
                [to_chip(made[2 * h + i], lambda c, a=a: c ^ a, chips) for i in range(2)]
                for h, (_, a, _) in enumerate(runs)
            ]
            targets = [
                dict(rows=run, chip=lambda c, b=b: c ^ b, extra=[(h, None)]) for h, (run, _, b) in enumerate(runs)
            ]
            made = sums(grads, core_in, [g[1] for g in got], rows, width, chips, targets, "second_sum")
            last = [to_chip(made[h], lambda c, b=b: c ^ b, chips) for h, (_, _, b) in enumerate(runs)]
            extra = [g[0] for g in got] + last
            parts = [dict(rows=run, extra=[(h, None), (2 + h, None)]) for h, (run, _, _) in enumerate(runs)]
        else:
            moves = [lambda c, m=m: (c + m) % chips for m in range(1, chips)]
            targets = [dict(rows=(0, per), chip=lambda c, m=m: lax.rem(c + m, chips), extra=[]) for m in range(1, chips)]
            made = sums(grads, core_in, [], rows, width, chips, targets, "first_sum")
            extra = [to_chip(x, move, chips) for x, move in zip(made, moves)]
            parts = [dict(rows=(0, per), extra=[(i, None) for i in range(chips - 1)])]
        kept, *sends = group_sum(grads, core_in, extra, rows, width, chips, parts)
        arrived = [to_group(x, s + 1, outer) for s, x in enumerate(sends)]
        totals.append((kept, *arrived))
        w = weights(kept, arrived, rows, master, first, second)
        own.append(w)
        received.append([to_group(w, s, outer) for s in range(1, outer)])

    new = finish(totals, spans, master, first, second)
    copy = assemble(own, received, spans, outer, owned).reshape(depth, width)
    return (*new, copy)


def solution(mesh):
    return jax.shard_map(
        functools.partial(body, inner=mesh.shape["inner"], outer=mesh.shape["outer"]),
        mesh=mesh,
        in_specs=(
            P("inner", "outer", None, None),
            P("outer", "inner"),
            P("outer", "inner"),
            P("outer", "inner"),
        ),
        out_specs=(P("outer", "inner"), P("outer", "inner"), P("outer", "inner"), P(None, "inner")),
        check_vma=False,
    )
```

```python
import functools

import jax
import jax.numpy as jnp
from jax import lax
from jax.experimental import pallas as pl
from jax.experimental.pallas import tpu as pltpu
from jax.sharding import PartitionSpec as P

beta_first = 0.9
beta_second = 0.95
learn_rate = 0.05
decay_rate = 0.1
adam_eps = 1e-05
bias_first = 1.0 - 0.9**10
bias_second = 1.0 - 0.95**10

CORES = 2
SUPERS = 2
STEP = 16
ANY = pl.BlockSpec(memory_space=pl.ANY)
VMEM = pl.BlockSpec(memory_space=pltpu.VMEM)


def local_kernel(kernel, out_shape, operands, name, in_specs=None, out_specs=None, sems=0):
    if in_specs is None:
        in_specs = [VMEM] * len(operands)
    if out_specs is None:
        out_specs = jax.tree.map(lambda _: VMEM, out_shape)
    nbytes = sum(s.size * s.dtype.itemsize for s in jax.tree.leaves(out_shape)) * 3
    return pl.pallas_call(
        kernel,
        out_shape=out_shape,
        in_specs=in_specs,
        out_specs=out_specs,
        scratch_shapes=[pltpu.SemaphoreType.DMA((sems,))] if sems else [],
        compiler_params=pltpu.CompilerParams(vmem_limit_bytes=4 << 20),
        cost_estimate=pl.CostEstimate(flops=nbytes, bytes_accessed=nbytes, transcendentals=0),
        name=name,
    )(*operands)


def bf16(*shape):
    return jax.ShapeDtypeStruct(shape, jnp.bfloat16)


def place():
    me = lax.axis_index("inner")
    return me // CORES, lax.rem(me, CORES)


def transfer(sources, targets, sems):
    copies = [pltpu.make_async_copy(s, d, sems.at[i]) for i, (s, d) in enumerate(zip(sources, targets))]
    for copy in copies:
        copy.start()
    for copy in copies:
        copy.wait()


def load(grads, parts, width, chips, name):
    outer = grads.shape[0]

    def kernel(grad_ref, *refs):
        *outs, sems = refs
        _, core = place()
        sources, targets = [], []
        for ((base, depth), side), out in zip(parts, outs):
            for chip in range(chips):
                block = CORES * chip + (1 - core if side else core)
                start = pl.multiple_of(block * width, width)
                sources.append(grad_ref.at[:, pl.ds(base, depth), pl.ds(start, width)])
                targets.append(out.at[chip])
        transfer(sources, targets, sems)

    shapes = [bf16(chips, outer, depth, width) for (_, depth), _ in parts]
    return local_kernel(kernel, shapes, [grads], name, in_specs=[ANY], sems=chips * len(parts))


def sum_of(terms):
    value = terms[0].astype(jnp.float32)
    for term in terms[1:]:
        value = value + term.astype(jnp.float32)
    return value


def each_step(blocks, depth, do):
    per = depth // STEP

    def step(i, carry):
        do(i // per, lax.rem(i, per) * STEP)
        return carry

    lax.fori_loop(0, blocks * per, step, 0)


def rows_at(start):
    return pl.ds(pl.multiple_of(start, STEP), STEP)


def chip_sums(grads, core_in, runs, name):
    _, outer, _, width = grads.shape

    def kernel(grad_ref, core_ref, *outs):
        chip, _ = place()
        for (base, depth, targets), out in zip(runs, outs):
            for at, target in enumerate(targets):
                to = target(chip)

                def do(block, start, at=at, to=to, base=base, out=out):
                    here = rows_at(base + start)
                    value = sum_of([grad_ref[to, block, here], core_ref[to, block, here]])
                    out[at, block, rows_at(start)] = value.astype(out.dtype)

                each_step(outer, depth, do)

    shapes = [bf16(len(targets), outer, depth, width) for _, depth, targets in runs]
    return local_kernel(kernel, shapes, [grads, core_in], name)


def pair_sums(grads, core_in, got, runs, name):
    _, outer, _, width = grads.shape

    def kernel(grad_ref, core_ref, *refs):
        chip, _ = place()
        for (base, depth, target), got_ref, out in zip(runs, refs, refs[len(got) :]):
            to = target(chip)

            def do(block, start, to=to, base=base, out=out, got_ref=got_ref):
                here, there = rows_at(base + start), rows_at(start)
                value = sum_of([grad_ref[to, block, here], core_ref[to, block, here], got_ref[1, block, there]])
                out[block, there] = value.astype(out.dtype)

            each_step(outer, depth, do)

    shapes = [bf16(outer, depth, width) for _, depth, _ in runs]
    return local_kernel(kernel, shapes, [grads, core_in, *got], name)


def group_sum(grads, core_in, extra, runs, name):
    _, outer, depth, width = grads.shape

    def kernel(grad_ref, core_ref, *refs):
        extra_refs, outs = refs[: len(extra)], refs[len(extra) :]
        chip, _ = place()
        here = lax.axis_index("outer")
        for shift in list(range(1, outer)) + [0]:
            block = lax.rem(here + shift, outer)
            for base, size, terms in runs:

                def do(_, start, block=block, base=base, terms=terms, out=outs[shift]):
                    rows = rows_at(base + start)
                    values = [grad_ref[chip, block, rows], core_ref[chip, block, rows]]
                    values += [
                        extra_refs[i][block, rows_at(start)] if j is None else extra_refs[i][j, block, rows_at(start)]
                        for i, j in terms
                    ]
                    out[rows] = sum_of(values).astype(out.dtype)

                each_step(1, size, do)

    shapes = [jax.ShapeDtypeStruct((depth, width), jnp.bfloat16 if s else jnp.float32) for s in range(outer)]
    return local_kernel(kernel, shapes, [grads, core_in, *extra], name)


def adam(total, master, first, second):
    new_first = beta_first * first + (1.0 - beta_first) * total
    new_second = beta_second * second + (1.0 - beta_second) * total * total
    update = new_first / bias_first / (jnp.sqrt(new_second / bias_second) + adam_eps) + decay_rate * master
    return master - learn_rate * update, new_first, new_second


def weights(terms, span, state, name):
    base, depth = span

    def kernel(*refs):
        *term_refs, master_ref, first_ref, second_ref, out = refs

        def do(_, start):
            here, there = rows_at(start), rows_at(base + start)
            total = sum_of([ref[here] for ref in term_refs])
            out[here] = adam(total, master_ref[there], first_ref[there], second_ref[there])[0].astype(out.dtype)

        each_step(1, depth, do)

    return local_kernel(kernel, bf16(depth, terms[0].shape[1]), [*terms, *state], name)


def finish(groups, spans, state):
    n = len(groups[0])

    def kernel(*refs):
        master_ref, first_ref, second_ref, *outs = refs[n * len(spans) :]
        for k, (base, depth) in enumerate(spans):

            def do(_, start, k=k, base=base):
                here, there = rows_at(start), rows_at(base + start)
                total = sum_of([ref[here] for ref in refs[n * k : n * k + n]])
                for out, value in zip(outs, adam(total, master_ref[there], first_ref[there], second_ref[there])):
                    out[there] = value

            each_step(1, depth, do)

    shapes = [jax.ShapeDtypeStruct(state[0].shape, jnp.float32)] * 3
    return local_kernel(kernel, shapes, [t for group in groups for t in group] + list(state), "finish")


def assemble(groups, spans, outer, owned):
    width = groups[0][0].shape[1]

    def kernel(*refs):
        *pieces, out, sems = refs
        here = lax.axis_index("outer")
        targets = [
            out.at[lax.rem(here + outer - shift, outer), pl.ds(base, depth)]
            for base, depth in spans
            for shift in range(outer)
        ]
        transfer(pieces, targets, sems)

    operands = [piece for group in groups for piece in group]
    return local_kernel(
        kernel, bf16(outer, owned, width), operands, "assemble", out_specs=ANY, sems=len(operands)
    )


def to_chip(x, target, chips):
    pairs = [(CORES * c + k, CORES * target(c) + k) for c in range(chips) for k in range(CORES)]
    return lax.ppermute(x, "inner", pairs)


def to_group(x, shift, outer):
    return lax.ppermute(x, "outer", [(i, (i + shift) % outer) for i in range(outer)])


def flip(mask):
    return lambda chip: chip ^ mask


def onward(shift, chips):
    return lambda chip: (chip + shift) % chips


def body(gradients, master, first, second, *, inner, outer):
    depth, columns = gradients.shape[2:]
    chips, owned, width = inner // CORES, depth // outer, columns // inner
    grads = gradients.reshape(outer, owned, columns)
    state = (master, first, second)

    supers = SUPERS if owned % (2 * STEP * SUPERS) == 0 else 1
    per = owned // supers
    spans = [(k * per, per) for k in range(supers)]
    two_steps = chips == 4 and per % (2 * STEP) == 0

    theirs = [load(grads, [(span, 1)], width, chips, "load_theirs")[0] for span in spans]
    mine = [load(grads, [(span, 0)], width, chips, "load_mine")[0] for span in spans]
    core_in = [lax.ppermute(x, "inner", [(i, i ^ 1) for i in range(inner)]) for x in theirs]

    totals, copies = [], []
    for k, span in enumerate(spans):
        if two_steps:
            half = per // 2
            links = [(0, 1, 2), (half, 2, 1)]
            runs = [(base, half, (flip(a), flip(a ^ b))) for base, a, b in links]
            made = chip_sums(mine[k], core_in[k], runs, "first_sum")
            got = [to_chip(x, flip(a), chips) for x, (_, a, _) in zip(made, links)]
            runs = [(base, half, flip(b)) for base, _, b in links]
            made = pair_sums(mine[k], core_in[k], got, runs, "second_sum")
            last = [to_chip(x, flip(b), chips) for x, (_, _, b) in zip(made, links)]
            extra = got + last
            runs = [(base, half, [(h, 0), (2 + h, None)]) for h, (base, _, _) in enumerate(links)]
        else:
            moves = [onward(m, chips) for m in range(1, chips)]
            made = chip_sums(mine[k], core_in[k], [(0, per, (move,)) for move in moves], "first_sum")
            extra = [to_chip(x, move, chips) for x, move in zip(made, moves)]
            runs = [(0, per, [(i, 0) for i in range(chips - 1)])]
        kept, *sends = group_sum(mine[k], core_in[k], extra, runs, "group_sum")
        totals.append((kept, *[to_group(x, s + 1, outer) for s, x in enumerate(sends)]))
        new = weights(totals[k], span, state, "weights")
        copies.append((new, *[to_group(new, s, outer) for s in range(1, outer)]))

    results = finish(totals, spans, state)
    return (*results, assemble(copies, spans, outer, owned).reshape(depth, columns // inner))


def solution(mesh):
    return jax.shard_map(
        functools.partial(body, inner=mesh.shape["inner"], outer=mesh.shape["outer"]),
        mesh=mesh,
        in_specs=(
            P("inner", "outer", None, None),
            P("outer", "inner"),
            P("outer", "inner"),
            P("outer", "inner"),
        ),
        out_specs=(P("outer", "inner"), P("outer", "inner"), P("outer", "inner"), P(None, "inner")),
        check_vma=False,
    )
```

```python
import functools

import jax
import jax.numpy as jnp
from jax import lax
from jax.experimental import pallas as pl
from jax.experimental.pallas import tpu as pltpu
from jax.sharding import PartitionSpec as P

beta_first = 0.9
beta_second = 0.95
learn_rate = 0.05
decay_rate = 0.1
adam_eps = 1e-05
bias_first = 1.0 - 0.9**10
bias_second = 1.0 - 0.95**10

CORES = 2
STEP = 16
LANES = 128
EIGHTHS = ((2, 2), (2, 2))
HALVE = (True, False)
ANY = pl.BlockSpec(memory_space=pl.ANY)
VMEM = pl.BlockSpec(memory_space=pltpu.VMEM)


def local_kernel(kernel, out_shape, operands, name, in_specs=None, out_specs=None, sems=0, after=(), grant=4):
    if in_specs is None:
        in_specs = [VMEM] * len(operands)
    if out_specs is None:
        out_specs = jax.tree.map(lambda _: VMEM, out_shape)
    n = len(operands)

    def ordered(*refs):
        kernel(*refs[:n], *refs[n + len(after) :])

    nbytes = sum(s.size * s.dtype.itemsize for s in jax.tree.leaves(out_shape)) * 3
    return pl.pallas_call(
        ordered,
        out_shape=out_shape,
        in_specs=in_specs + [ANY] * len(after),
        out_specs=out_specs,
        scratch_shapes=[pltpu.SemaphoreType.DMA((sems,))] if sems else [],
        compiler_params=pltpu.CompilerParams(vmem_limit_bytes=grant << 20),
        cost_estimate=pl.CostEstimate(flops=nbytes, bytes_accessed=nbytes, transcendentals=0),
        name=name,
    )(*operands, *after)


def bf16(*shape):
    return jax.ShapeDtypeStruct(shape, jnp.bfloat16)


def f32(*shape):
    return jax.ShapeDtypeStruct(shape, jnp.float32)


def place():
    me = lax.axis_index("inner")
    return me // CORES, lax.rem(me, CORES), lax.axis_index("outer")


def transfer(sources, targets, sems):
    copies = [pltpu.make_async_copy(s, d, sems.at[i]) for i, (s, d) in enumerate(zip(sources, targets))]
    for copy in copies:
        copy.start()
    for copy in copies:
        copy.wait()


def load(grads, span, side, width, chips, name, after=(), grant=4):
    outer, owned, _ = grads.shape
    base, size = span

    def kernel(grad_ref, out, sems):
        core = place()[1]
        sources = []
        for chip in range(chips):
            block = CORES * chip + (1 - core if side else core)
            sources.append(grad_ref.at[:, :, pl.ds(pl.multiple_of(block * width + base, LANES), size)])
        transfer(sources, [out.at[chip] for chip in range(chips)], sems)

    shape = bf16(chips, outer, owned, size)
    return local_kernel(kernel, shape, [grads], name, in_specs=[ANY], sems=chips, after=after, grant=grant)


def rows_at(start):
    return pl.ds(pl.multiple_of(start, STEP), STEP)


def each_step(depth, do):
    lax.fori_loop(0, depth // STEP, lambda i, carry: (do(rows_at(i * STEP)), carry)[1], 0, unroll=True)


def sum_of(terms, rows):
    value = None
    for ref, index in terms:
        term = ref[(*index, rows)].astype(jnp.float32)
        value = term if value is None else value + term
    return value


def sums(operands, shapes, plan, name, after=()):
    def kernel(*refs):
        outs = refs[len(operands) :]
        for out, pieces in zip(outs, plan(refs[: len(operands)], *place())):
            for index, columns, terms in pieces:

                def do(rows, out=out, index=index, columns=columns, terms=terms):
                    out[(*index, rows, columns)] = sum_of(terms, rows).astype(out.dtype)

                each_step(out.shape[-2], do)

    return local_kernel(kernel, shapes, operands, name, after=after)


def adam(total, master, first, second):
    new_first = beta_first * first + (1.0 - beta_first) * total
    new_second = beta_second * second + (1.0 - beta_second) * total * total
    update = new_first / bias_first / (jnp.sqrt(new_second / bias_second) + adam_eps) + decay_rate * master
    return master - learn_rate * update, new_first, new_second


def weights(total, span, state, name, after=()):
    arrays, indices = zip(*total)
    shape = arrays[0].shape[-2:]
    columns = pl.ds(*span)

    def kernel(*refs):
        *terms, master_ref, first_ref, second_ref, out = refs

        def do(rows):
            value = sum_of(list(zip(terms, indices)), rows)
            value, _, _ = adam(value, master_ref[rows, columns], first_ref[rows, columns], second_ref[rows, columns])
            out[rows] = value.astype(out.dtype)

        each_step(shape[0], do)

    return local_kernel(kernel, bf16(*shape), [*arrays, *state], name, after=after)


def finish(totals, spans, state):
    arrays = [array for total in totals for array, _ in total]
    n = len(arrays)

    def kernel(*refs):
        state_refs, outs = refs[n : n + 3], refs[n + 3 :]
        at = 0
        for span, total in zip(spans, totals):
            columns = pl.ds(*span)
            terms = [(ref, index) for ref, (_, index) in zip(refs[at : at + len(total)], total)]
            at += len(total)

            def do(rows, terms=terms, columns=columns):
                values = adam(sum_of(terms, rows), *[ref[rows, columns] for ref in state_refs])
                for out, value in zip(outs, values):
                    out[rows, columns] = value

            each_step(state[0].shape[0], do)

    return local_kernel(kernel, [f32(*state[0].shape)] * 3, arrays + list(state), "finish")


def assemble(groups, sources, spans, outer, width):
    def kernel(*refs):
        *pieces, out, sems = refs
        here = lax.axis_index("outer")
        targets = [out.at[source(here), :, pl.ds(*span)] for span in spans for source in sources]
        transfer(pieces, targets, sems)

    operands = [piece for group in groups for piece in group]
    shape = bf16(outer, operands[0].shape[0], width)
    return local_kernel(kernel, shape, operands, "assemble", out_specs=ANY, sems=len(operands))


def to_core(x, inner):
    return lax.ppermute(x, "inner", [(i, i ^ 1) for i in range(inner)])


def to_chip(x, target, chips):
    pairs = [(CORES * c + k, CORES * target(c, k) + k) for c in range(chips) for k in range(CORES)]
    return lax.ppermute(x, "inner", pairs)


def to_group(x, target, inner, outer):
    pairs = [(i * outer + z, i * outer + target(z, i % CORES)) for i in range(inner) for z in range(outer)]
    return lax.ppermute(x, ("inner", "outer"), pairs)


def local(mine, core_in, chip, block):
    return [(mine, (chip, block)), (core_in, (chip, block))]


EVERY = slice(None)


def plain_total(mine, core_in, inner, outer):
    chips, _, depth, width = mine.shape
    moves = [lambda chip, core, m=m: (chip + m) % chips for m in range(1, chips)]
    steps = [lambda z, core, s=s: (z + s) % outer for s in range(1, outer)]

    def first(refs, chip, core, here):
        return [[((z,), EVERY, local(*refs, move(chip, core), z)) for z in range(outer)] for move in moves]

    made = sums([mine, core_in], [bf16(outer, depth, width)] * len(moves), first, "first_sum")
    got = [to_chip(x, move, chips) for x, move in zip(made, moves)]

    def group(refs, chip, core, here):
        blocks = [here] + [step(here, core) for step in steps]
        return [[((), EVERY, local(*refs[:2], chip, z) + [(ref, (z,)) for ref in refs[2:]])] for z in blocks]

    shapes = [f32(depth, width)] + [bf16(depth, width)] * len(steps)
    kept, *sends = sums([mine, core_in, *got], shapes, group, "group_sum")
    return [(kept, ())] + [(to_group(x, step, inner, outer), ()) for x, step in zip(sends, steps)]


CHIP_STEPS = [lambda chip, core: chip ^ (1 + core), lambda chip, core: chip ^ (2 - core)]
OUTER_STEPS = [lambda z, core: z ^ 1, lambda z, core: z ^ 3]


def over_group(mine, core_in, chips):
    _, outer, depth, width = mine.shape

    def first(refs, chip, core, here):
        targets = [CHIP_STEPS[0](chip, core), chip ^ 3]
        return [[((i, z), EVERY, local(*refs, to, z)) for i, to in enumerate(targets) for z in range(outer)]]

    [made] = sums([mine, core_in], [bf16(2, outer, depth, width)], first, "first_sum")
    got = to_chip(made, CHIP_STEPS[0], chips)

    def second(refs, chip, core, here):
        to = CHIP_STEPS[1](chip, core)
        return [[((z,), EVERY, local(*refs[:2], to, z) + [(refs[2], (1, z))]) for z in range(outer)]]

    after = yield
    [made] = sums([mine, core_in, got], [bf16(outer, depth, width)], second, "second_sum", after)
    yield mine, core_in, got, to_chip(made, CHIP_STEPS[1], chips)


def group_pieces(pieces, refs, chip, z, index, more=()):
    out, at = [], 0
    for k in range(len(pieces)):
        mine, core_in, got, last = refs[4 * k : 4 * k + 4]
        columns = pl.ds(at, mine.shape[-1])
        at += mine.shape[-1]
        terms = local(mine, core_in, chip, z) + [(got, (0, z)), (last, (z,))]
        out.append((index, columns, terms + [(ref.at[..., columns], lead) for ref, lead in more]))
    return out


def halve_groups(pieces, inner, outer):
    depth, width = pieces[0][0].shape[2], sum(piece[0].shape[3] for piece in pieces)
    arrays = [array for piece in pieces for array in piece]

    def first(refs, chip, core, here):
        targets = [OUTER_STEPS[0](here, core), here ^ 2]
        return [[p for i, to in enumerate(targets) for p in group_pieces(pieces, refs, chip, to, (i,))]]

    [begun] = sums(arrays, [bf16(2, depth, width)], first, "halve")
    got = to_group(begun, OUTER_STEPS[0], inner, outer)

    def second(refs, chip, core, here):
        to = OUTER_STEPS[1](here, core)
        return [
            group_pieces(pieces, refs, chip, here, (), [(refs[-1], (0,))]),
            group_pieces(pieces, refs, chip, to, (), [(refs[-1], (1,))]),
        ]

    kept, made = sums([*arrays, got], [f32(depth, width), bf16(depth, width)], second, "halve_again")
    return [(kept, ()), (to_group(made, OUTER_STEPS[1], inner, outer), ())], begun


def direct_groups(pieces, inner, outer):
    depth, width = pieces[0][0].shape[2], sum(piece[0].shape[3] for piece in pieces)
    arrays = [array for piece in pieces for array in piece]
    masks = [2, 3, 1]

    def group(refs, chip, core, here):
        return [group_pieces(pieces, refs, chip, here ^ m, ()) for m in [0] + masks]

    shapes = [f32(depth, width)] + [bf16(depth, width)] * len(masks)
    kept, *sends = sums(arrays, shapes, group, "group_sum")
    return [(kept, ())] + [(to_group(x, lambda z, _, m=m: z ^ m, inner, outer), ()) for x, m in zip(sends, masks)], kept


def gather(own, inner, outer):
    if outer == 4:
        far, diag, near = [to_group(own, lambda z, _, m=m: z ^ m, inner, outer) for m in (2, 3, 1)]
        return own, near, far, diag
    return own, *[to_group(own, lambda z, _, s=s: (z + s) % outer, inner, outer) for s in range(1, outer)]


def body(gradients, master, first, second, *, inner, outer):
    depth, columns = gradients.shape[2:]
    chips, owned, width = inner // CORES, depth // outer, columns // inner
    grads = gradients.reshape(outer, owned, columns)
    state = (master, first, second)

    if chips == 4 and outer == 4 and width % (8 * LANES) == 0:
        sizes = [n * width // 8 for span in EIGHTHS for n in span]
        parts = [(sum(sizes[:k]), size) for k, size in enumerate(sizes)]
        theirs = [load(grads, part, 1, width, chips, "load_theirs", grant=4 if k else 52) for k, part in enumerate(parts)]
        core_in = [to_core(x, inner) for x in theirs]
        mine = [load(grads, part, 0, width, chips, "load_mine") for part in parts]
        ways = [over_group(m, c, chips) for m, c in zip(mine, core_in)]
        for way in ways:
            next(way)
        sources = [lambda z, m=m: z ^ m for m in range(4)]
        spans, totals, at, begun = [], [], 0, []
        for k, span in enumerate(EIGHTHS):
            after = [[]] * (len(span) - 1) + [begun]
            some = [way.send(after[n]) for n, way in enumerate(ways[at : at + len(span)])]
            spans.append((parts[at][0], sum(sizes[at : at + len(span)])))
            at += len(span)
            total, first_made = (halve_groups if HALVE[k] else direct_groups)(some, inner, outer)
            totals.append(total)
            begun = [first_made]
    else:
        spans = [(0, width)]
        sources = [lambda z, s=s: (z + outer - s) % outer for s in range(outer)]
        theirs, mine = [load(grads, spans[0], side, width, chips, "load") for side in (1, 0)]
        totals = [plain_total(mine, to_core(theirs, inner), inner, outer)]

    made = [weights(total, span, state, "weights") for total, span in zip(totals, spans)]
    copy = assemble([gather(new, inner, outer) for new in made], sources, spans, outer, width)
    return (*finish(totals, spans, state), copy.reshape(depth, width))


def solution(mesh):
    return jax.shard_map(
        functools.partial(body, inner=mesh.shape["inner"], outer=mesh.shape["outer"]),
        mesh=mesh,
        in_specs=(
            P("inner", "outer", None, None),
            P("outer", "inner"),
            P("outer", "inner"),
            P("outer", "inner"),
        ),
        out_specs=(P("outer", "inner"), P("outer", "inner"), P("outer", "inner"), P(None, "inner")),
        check_vma=False,
    )
```

```python
import functools

import jax
import jax.numpy as jnp
from jax import lax
from jax.experimental import pallas as pl
from jax.experimental.pallas import tpu as pltpu
from jax.sharding import PartitionSpec as P

beta_first = 0.9
beta_second = 0.95
learn_rate = 0.05
decay_rate = 0.1
adam_eps = 1e-05
bias_first = 1.0 - 0.9**10
bias_second = 1.0 - 0.95**10

CORES = 2
STEP = 16
LANES = 128
ANY = pl.BlockSpec(memory_space=pl.ANY)
VMEM = pl.BlockSpec(memory_space=pltpu.VMEM)


def local_kernel(kernel, out_shape, operands, name, in_specs=None, out_specs=None, sems=0, after=(), grant=4):
    if in_specs is None:
        in_specs = [VMEM] * len(operands)
    if out_specs is None:
        out_specs = jax.tree.map(lambda _: VMEM, out_shape)
    n = len(operands)

    def ordered(*refs):
        kernel(*refs[:n], *refs[n + len(after) :])

    nbytes = sum(s.size * s.dtype.itemsize for s in jax.tree.leaves(out_shape)) * 3
    return pl.pallas_call(
        ordered,
        out_shape=out_shape,
        in_specs=in_specs + [ANY] * len(after),
        out_specs=out_specs,
        scratch_shapes=[pltpu.SemaphoreType.DMA((sems,))] if sems else [],
        compiler_params=pltpu.CompilerParams(vmem_limit_bytes=grant << 20),
        cost_estimate=pl.CostEstimate(flops=nbytes, bytes_accessed=nbytes, transcendentals=0),
        name=name,
    )(*operands, *after)


def bf16(*shape):
    return jax.ShapeDtypeStruct(shape, jnp.bfloat16)


def f32(*shape):
    return jax.ShapeDtypeStruct(shape, jnp.float32)


def place():
    me = lax.axis_index("inner")
    return me // CORES, lax.rem(me, CORES), lax.axis_index("outer")


def transfer(sources, targets, sems):
    copies = [pltpu.make_async_copy(s, d, sems.at[i]) for i, (s, d) in enumerate(zip(sources, targets))]
    for copy in copies:
        copy.start()
    for copy in copies:
        copy.wait()


def load(grads, span, side, width, chips, name, after=(), grant=4):
    outer, owned, _ = grads.shape
    base, size = span

    def kernel(grad_ref, out, sems):
        core = place()[1]
        sources = []
        for chip in range(chips):
            block = CORES * chip + (1 - core if side else core)
            sources.append(grad_ref.at[:, :, pl.ds(pl.multiple_of(block * width + base, LANES), size)])
        transfer(sources, [out.at[chip] for chip in range(chips)], sems)

    shape = bf16(chips, outer, owned, size)
    return local_kernel(kernel, shape, [grads], name, in_specs=[ANY], sems=chips, after=after, grant=grant)


def rows_at(start):
    return pl.ds(pl.multiple_of(start, STEP), STEP)


def each_step(depth, do):
    lax.fori_loop(0, depth // STEP, lambda i, carry: (do(rows_at(i * STEP)), carry)[1], 0, unroll=True)


def sum_of(terms, rows):
    value = None
    for ref, index in terms:
        term = ref[(*index, rows)].astype(jnp.float32)
        value = term if value is None else value + term
    return value


def sums(operands, shapes, plan, name, after=()):
    def kernel(*refs):
        outs = refs[len(operands) :]
        for out, pieces in zip(outs, plan(refs[: len(operands)], *place())):
            for index, columns, terms in pieces:

                def do(rows, out=out, index=index, columns=columns, terms=terms):
                    out[(*index, rows, columns)] = sum_of(terms, rows).astype(out.dtype)

                each_step(out.shape[-2], do)

    return local_kernel(kernel, shapes, operands, name, after=after)


def adam(total, master, first, second):
    new_first = beta_first * first + (1.0 - beta_first) * total
    new_second = beta_second * second + (1.0 - beta_second) * total * total
    update = new_first / bias_first / (jnp.sqrt(new_second / bias_second) + adam_eps) + decay_rate * master
    return master - learn_rate * update, new_first, new_second


def each_piece(total, refs, base=0):
    refs = list(refs)
    for size, terms in total:
        yield pl.ds(base, size), [(refs.pop(0), index) for _, index in terms]
        base += size


def arrays_of(total):
    return [array for _, terms in total for array, _ in terms]


def weights(total, span, state, name, after=()):
    arrays = arrays_of(total)
    depth = state[0].shape[0]

    def kernel(*refs):
        state_refs, out = refs[len(arrays) : -1], refs[-1]
        for columns, terms in each_piece(total, refs, span[0]):
            here = pl.ds(columns.start - span[0], columns.size)

            def do(rows, terms=terms, columns=columns, here=here):
                value, _, _ = adam(sum_of(terms, rows), *[ref[rows, columns] for ref in state_refs])
                out[rows, here] = value.astype(out.dtype)

            each_step(depth, do)

    return local_kernel(kernel, bf16(depth, span[1]), [*arrays, *state], name, after=after)


def finish(totals, state):
    total = [piece for pieces in totals for piece in pieces]
    arrays = arrays_of(total)
    n = len(arrays)

    def kernel(*refs):
        state_refs, outs = refs[n : n + 3], refs[n + 3 :]
        for columns, terms in each_piece(total, refs):

            def do(rows, terms=terms, columns=columns):
                values = adam(sum_of(terms, rows), *[ref[rows, columns] for ref in state_refs])
                for out, value in zip(outs, values):
                    out[rows, columns] = value

            each_step(state[0].shape[0], do)

    return local_kernel(kernel, [f32(*state[0].shape)] * 3, arrays + list(state), "finish")


def assemble(groups, sources, spans, outer, width):
    def kernel(*refs):
        *pieces, out, sems = refs
        here = lax.axis_index("outer")
        targets = [out.at[source(here), :, pl.ds(*span)] for span in spans for source in sources]
        transfer(pieces, targets, sems)

    operands = [piece for group in groups for piece in group]
    shape = bf16(outer, operands[0].shape[0], width)
    return local_kernel(kernel, shape, operands, "assemble", out_specs=ANY, sems=len(operands))


def to_core(x, inner):
    return lax.ppermute(x, "inner", [(i, i ^ 1) for i in range(inner)])


def to_chip(x, target, chips):
    pairs = [(CORES * c + k, CORES * target(c, k) + k) for c in range(chips) for k in range(CORES)]
    return lax.ppermute(x, "inner", pairs)


def to_group(x, target, inner, outer):
    pairs = [(i * outer + z, i * outer + target(z, i % CORES)) for i in range(inner) for z in range(outer)]
    return lax.ppermute(x, ("inner", "outer"), pairs)


def local(mine, core_in, chip, block):
    return [(mine, (chip, block)), (core_in, (chip, block))]


EVERY = slice(None)


def plain_total(mine, core_in, inner, outer):
    chips, _, depth, width = mine.shape
    moves = [lambda chip, core, m=m: (chip + m) % chips for m in range(1, chips)]
    steps = [lambda z, core, s=s: (z + s) % outer for s in range(1, outer)]

    def first(refs, chip, core, here):
        return [[((z,), EVERY, local(*refs, move(chip, core), z)) for z in range(outer)] for move in moves]

    made = sums([mine, core_in], [bf16(outer, depth, width)] * len(moves), first, "first_sum")
    got = [to_chip(x, move, chips) for x, move in zip(made, moves)]

    def group(refs, chip, core, here):
        blocks = [here] + [step(here, core) for step in steps]
        return [[((), EVERY, local(*refs[:2], chip, z) + [(ref, (z,)) for ref in refs[2:]])] for z in blocks]

    shapes = [f32(depth, width)] + [bf16(depth, width)] * len(steps)
    kept, *sends = sums([mine, core_in, *got], shapes, group, "group_sum")
    return [(kept, ())] + [(to_group(x, step, inner, outer), ()) for x, step in zip(sends, steps)]


CHIP_STEPS = [lambda chip, core: chip ^ (1 + core), lambda chip, core: chip ^ (2 - core)]
OUTER_STEPS = [lambda z, core: z ^ 1, lambda z, core: z ^ 3]
PARTNERS = [2, 3, 1]


def group_pieces(parts, refs, chip, z, index, more=()):
    out, at = [], 0
    for k, (mine, *_) in enumerate(parts):
        mine_ref, core_ref, got, last = refs[4 * k : 4 * k + 4]
        columns = pl.ds(at, mine.shape[-1])
        at += mine.shape[-1]
        terms = local(mine_ref, core_ref, chip, z) + [(got, (0, z)), (last, (z,))]
        out.append((index, columns, terms + [(ref.at[..., columns], lead) for ref, lead in more]))
    return out


def four_by_four(grads, width, inner, outer):
    chips = inner // CORES
    depth = grads.shape[1]
    widths = [width // 4] * 4
    wide = widths[0] + widths[1]
    order, last = [], {}
    parts = [[None, None] for _ in widths]

    def run(arrays, shapes, plan, name):
        made = sums(arrays, shapes, plan, name, order[-1:])
        order.append(made[0])
        return made

    def chip_targets(chip, core):
        return list(enumerate([CHIP_STEPS[0](chip, core), chip ^ 3]))

    def outer_targets(here, core):
        return list(enumerate([OUTER_STEPS[0](here, core), here ^ 2]))

    def over_chips(k):
        def plan(refs, chip, core, here):
            return [[((i, z), EVERY, local(*refs, to, z)) for i, to in chip_targets(chip, core) for z in range(outer)]]

        [made] = run(parts[k], [bf16(2, outer, depth, widths[k])], plan, "first_sum")
        parts[k].append(to_chip(made, CHIP_STEPS[0], chips))

    def over_chips_again(k):
        def plan(refs, chip, core, here):
            to = CHIP_STEPS[1](chip, core)
            return [[((z,), EVERY, local(*refs[:2], to, z) + [(refs[2], (1, z))]) for z in range(outer)]]

        [made] = run(parts[k], [bf16(outer, depth, widths[k])], plan, "second_sum")
        parts[k].append(to_chip(made, CHIP_STEPS[1], chips))

    def halve():
        def plan(refs, chip, core, here):
            return [[p for i, to in outer_targets(here, core) for p in group_pieces(parts[:2], refs, chip, to, (i,))]]

        [made] = run([*parts[0], *parts[1]], [bf16(2, depth, wide)], plan, "halve")
        last["halve"] = to_group(made, OUTER_STEPS[0], inner, outer)

    def halve_again():
        def plan(refs, chip, core, here):
            to = OUTER_STEPS[1](here, core)
            return [
                group_pieces(parts[:2], refs, chip, here, (), [(refs[-1], (0,))]),
                group_pieces(parts[:2], refs, chip, to, (), [(refs[-1], (1,))]),
            ]

        shapes = [f32(depth, wide), bf16(depth, wide)]
        kept, made = run([*parts[0], *parts[1], last["halve"]], shapes, plan, "halve_again")
        last["first"] = [(kept, ()), (to_group(made, OUTER_STEPS[1], inner, outer), ())]

    def group():
        def plan(refs, chip, core, here):
            return [group_pieces(parts[2:3], refs, chip, here ^ m, ()) for m in [0] + PARTNERS]

        shapes = [f32(depth, widths[2])] + [bf16(depth, widths[2])] * len(PARTNERS)
        kept, *sends = run(parts[2], shapes, plan, "group_sum")
        last["second"] = [(kept, ())]
        for x, m in zip(sends, PARTNERS):
            last["second"].append((to_group(x, lambda z, _, m=m: z ^ m, inner, outer), ()))

    def early():
        def plan(refs, chip, core, here):
            return [
                [((i, c), EVERY, local(*refs, c, to)) for i, to in outer_targets(here, core) for c in range(chips)]
            ]

        [made] = run(parts[3], [bf16(2, chips, depth, widths[3])], plan, "early_first")
        parts[3].append(to_group(made, OUTER_STEPS[0], inner, outer))

    def early_again():
        def plan(refs, chip, core, here):
            to = OUTER_STEPS[1](here, core)
            return [[((c,), EVERY, local(*refs[:2], c, to) + [(refs[2], (1, c))]) for c in range(chips)]]

        [made] = run(parts[3], [bf16(chips, depth, widths[3])], plan, "early_second")
        parts[3].append(to_group(made, OUTER_STEPS[1], inner, outer))

    def line(refs, c, here):
        return local(*refs[:2], c, here) + [(refs[2], (0, c)), (refs[3], (c,))]

    def early_chips():
        def plan(refs, chip, core, here):
            return [
                [((), EVERY, line(refs, chip, here))],
                [((i,), EVERY, line(refs, to, here)) for i, to in chip_targets(chip, core)],
            ]

        kept, made = run(parts[3], [f32(depth, widths[3]), bf16(2, depth, widths[3])], plan, "early_third")
        parts[3].append(to_chip(made, CHIP_STEPS[0], chips))
        last["third"] = [(kept, ()), (parts[3][4], (0,))]

    def early_chips_again():
        def plan(refs, chip, core, here):
            return [[((), EVERY, line(refs, CHIP_STEPS[1](chip, core), here) + [(refs[4], (1,))])]]

        [made] = run(parts[3], [bf16(depth, widths[3])], plan, "early_fourth")
        last["third"].append((to_chip(made, CHIP_STEPS[1], chips), ()))

    def theirs(k):
        place, grant = (sum(widths[:k]), widths[k]), 4 if order else 52
        order.append(load(grads, place, 1, width, chips, "load_theirs", order[-1:], grant))
        parts[k][1] = to_core(order[-1], inner)

    def ours(k):
        place = sum(widths[:k]), widths[k]
        order.append(load(grads, place, 0, width, chips, "load_mine", order[-1:]))
        parts[k][0] = order[-1]

    for k in (0, 3, 1, 2):
        theirs(k)
    ours(0)
    over_chips(0)
    ours(3)
    early()
    ours(1)
    over_chips(1)
    ours(2)
    over_chips(2)
    over_chips_again(0)
    early_again()
    over_chips_again(1)
    over_chips_again(2)
    halve()
    early_chips()
    group()
    halve_again()
    early_chips_again()
    return [[(wide, last["first"])], [(widths[2], last["second"]), (widths[3], last["third"])]]


def gather(own, inner, outer, straight):
    if outer == 4:
        if straight:
            pieces = {m: to_group(own, lambda z, _, m=m: z ^ m, inner, outer) for m in (2, 3, 1)}
        else:
            pieces = {m: to_group(own, lambda z, _, m=m: z ^ m, inner, outer) for m in (2, 1)}
            pieces[3] = to_group(pieces[2], lambda z, _: z ^ 1, inner, outer)
        return own, *[pieces[m] for m in (2, 1, 3)]
    return own, *[to_group(own, lambda z, _, s=s: (z + s) % outer, inner, outer) for s in range(1, outer)]


def body(gradients, master, first, second, *, inner, outer):
    depth, columns = gradients.shape[2:]
    chips, owned, width = inner // CORES, depth // outer, columns // inner
    grads = gradients.reshape(outer, owned, columns)
    state = (master, first, second)

    if chips == 4 and outer == 4 and width % (4 * LANES) == 0:
        totals = four_by_four(grads, width, inner, outer)
        sources = [lambda z, m=m: z ^ m for m in (0, 2, 1, 3)]
    else:
        sources = [lambda z, s=s: (z + outer - s) % outer for s in range(outer)]
        theirs, mine = [load(grads, (0, width), side, width, chips, "load") for side in (1, 0)]
        totals = [[(width, plain_total(mine, to_core(theirs, inner), inner, outer))]]

    sizes = [sum(size for size, _ in total) for total in totals]
    spans = [(sum(sizes[:k]), size) for k, size in enumerate(sizes)]
    made = [weights(total, span, state, "weights") for total, span in zip(totals, spans)]
    copy = assemble([gather(new, inner, outer, k == 0) for k, new in enumerate(made)], sources, spans, outer, width)
    return (*finish(totals, state), copy.reshape(depth, width))


def solution(mesh):
    return jax.shard_map(
        functools.partial(body, inner=mesh.shape["inner"], outer=mesh.shape["outer"]),
        mesh=mesh,
        in_specs=(
            P("inner", "outer", None, None),
            P("outer", "inner"),
            P("outer", "inner"),
            P("outer", "inner"),
        ),
        out_specs=(P("outer", "inner"), P("outer", "inner"), P("outer", "inner"), P(None, "inner")),
        check_vma=False,
    )
```

```python
import functools

import jax
import jax.numpy as jnp
from jax import lax
from jax.experimental import pallas as pl
from jax.experimental.pallas import tpu as pltpu
from jax.sharding import PartitionSpec as P

beta_first = 0.9
beta_second = 0.95
learn_rate = 0.05
decay_rate = 0.1
adam_eps = 1e-05
bias_first = 1.0 - 0.9**10
bias_second = 1.0 - 0.95**10

CORES = 2
STEP = 16
LANES = 128
ANY = pl.BlockSpec(memory_space=pl.ANY)
VMEM = pl.BlockSpec(memory_space=pltpu.VMEM)


def local_kernel(kernel, out_shape, operands, name, in_specs=None, out_specs=None, sems=0, after=(), grant=4):
    if in_specs is None:
        in_specs = [VMEM] * len(operands)
    if out_specs is None:
        out_specs = jax.tree.map(lambda _: VMEM, out_shape)
    n = len(operands)

    def ordered(*refs):
        kernel(*refs[:n], *refs[n + len(after) :])

    nbytes = sum(s.size * s.dtype.itemsize for s in jax.tree.leaves(out_shape)) * 3
    return pl.pallas_call(
        ordered,
        out_shape=out_shape,
        in_specs=in_specs + [ANY] * len(after),
        out_specs=out_specs,
        scratch_shapes=[pltpu.SemaphoreType.DMA((sems,))] if sems else [],
        compiler_params=pltpu.CompilerParams(vmem_limit_bytes=grant << 20),
        cost_estimate=pl.CostEstimate(flops=nbytes, bytes_accessed=nbytes, transcendentals=0),
        name=name,
    )(*operands, *after)


def bf16(*shape):
    return jax.ShapeDtypeStruct(shape, jnp.bfloat16)


def f32(*shape):
    return jax.ShapeDtypeStruct(shape, jnp.float32)


def place():
    me = lax.axis_index("inner")
    return me // CORES, lax.rem(me, CORES), lax.axis_index("outer")


def transfer(sources, targets, sems):
    copies = [pltpu.make_async_copy(s, d, sems.at[i]) for i, (s, d) in enumerate(zip(sources, targets))]
    for copy in copies:
        copy.start()
    for copy in copies:
        copy.wait()


def load(grads, span, side, width, chips, name, after=(), grant=4):
    outer, owned, _ = grads.shape
    base, size = span

    def kernel(grad_ref, out, sems):
        core = place()[1]
        sources = []
        for chip in range(chips):
            block = CORES * chip + (1 - core if side else core)
            sources.append(grad_ref.at[:, :, pl.ds(pl.multiple_of(block * width + base, LANES), size)])
        transfer(sources, [out.at[chip] for chip in range(chips)], sems)

    shape = bf16(chips, outer, owned, size)
    return local_kernel(kernel, shape, [grads], name, in_specs=[ANY], sems=chips, after=after, grant=grant)


def rows_at(start):
    return pl.ds(pl.multiple_of(start, STEP), STEP)


def each_step(depth, do):
    lax.fori_loop(0, depth // STEP, lambda i, carry: (do(rows_at(i * STEP)), carry)[1], 0, unroll=True)


def sum_of(terms, rows):
    value = None
    for ref, index in terms:
        term = ref[(*index, rows)].astype(jnp.float32)
        value = term if value is None else value + term
    return value


def sums(operands, shapes, plan, name, after=()):
    def kernel(*refs):
        outs = refs[len(operands) :]
        for out, pieces in zip(outs, plan(refs[: len(operands)], *place())):
            for index, columns, terms in pieces:

                def do(rows, out=out, index=index, columns=columns, terms=terms):
                    out[(*index, rows, columns)] = sum_of(terms, rows).astype(out.dtype)

                each_step(out.shape[-2], do)

    return local_kernel(kernel, shapes, operands, name, after=after)


def adam(total, master, first, second):
    new_first = beta_first * first + (1.0 - beta_first) * total
    new_second = beta_second * second + (1.0 - beta_second) * total * total
    update = new_first / bias_first / (jnp.sqrt(new_second / bias_second) + adam_eps) + decay_rate * master
    return master - learn_rate * update, new_first, new_second


def each_piece(total, refs, base=0):
    refs = list(refs)
    for size, terms in total:
        yield pl.ds(base, size), [(refs.pop(0), index) for _, index in terms]
        base += size


def arrays_of(total):
    return [array for _, terms in total for array, _ in terms]


def weights(total, span, state, name, after=()):
    arrays = arrays_of(total)
    depth = state[0].shape[0]

    def kernel(*refs):
        state_refs, out = refs[len(arrays) : -1], refs[-1]
        for columns, terms in each_piece(total, refs, span[0]):
            here = pl.ds(columns.start - span[0], columns.size)

            def do(rows, terms=terms, columns=columns, here=here):
                value, _, _ = adam(sum_of(terms, rows), *[ref[rows, columns] for ref in state_refs])
                out[rows, here] = value.astype(out.dtype)

            each_step(depth, do)

    return local_kernel(kernel, bf16(depth, span[1]), [*arrays, *state], name, after=after)


def finish(totals, state):
    total = [piece for pieces in totals for piece in pieces]
    arrays = arrays_of(total)
    n = len(arrays)

    def kernel(*refs):
        state_refs, outs = refs[n : n + 3], refs[n + 3 :]
        for columns, terms in each_piece(total, refs):

            def do(rows, terms=terms, columns=columns):
                values = adam(sum_of(terms, rows), *[ref[rows, columns] for ref in state_refs])
                for out, value in zip(outs, values):
                    out[rows, columns] = value

            each_step(state[0].shape[0], do)

    return local_kernel(kernel, [f32(*state[0].shape)] * 3, arrays + list(state), "finish")


def assemble(groups, sources, spans, outer, width):
    def kernel(*refs):
        *pieces, out, sems = refs
        here = lax.axis_index("outer")
        targets = [out.at[source(here), :, pl.ds(*span)] for span in spans for source in sources]
        transfer(pieces, targets, sems)

    operands = [piece for group in groups for piece in group]
    shape = bf16(outer, operands[0].shape[0], width)
    return local_kernel(kernel, shape, operands, "assemble", out_specs=ANY, sems=len(operands))


def to_core(x, inner):
    return lax.ppermute(x, "inner", [(i, i ^ 1) for i in range(inner)])


def to_chip(x, target, chips):
    pairs = [(CORES * c + k, CORES * target(c, k) + k) for c in range(chips) for k in range(CORES)]
    return lax.ppermute(x, "inner", pairs)


def to_group(x, target, inner, outer):
    pairs = [(i * outer + z, i * outer + target(z, i % CORES)) for i in range(inner) for z in range(outer)]
    return lax.ppermute(x, ("inner", "outer"), pairs)


def local(mine, core_in, chip, block):
    return [(mine, (chip, block)), (core_in, (chip, block))]


EVERY = slice(None)


def plain_total(mine, core_in, inner, outer):
    chips, _, depth, width = mine.shape
    moves = [lambda chip, core, m=m: (chip + m) % chips for m in range(1, chips)]
    steps = [lambda z, core, s=s: (z + s) % outer for s in range(1, outer)]

    def first(refs, chip, core, here):
        return [[((z,), EVERY, local(*refs, move(chip, core), z)) for z in range(outer)] for move in moves]

    made = sums([mine, core_in], [bf16(outer, depth, width)] * len(moves), first, "first_sum")
    got = [to_chip(x, move, chips) for x, move in zip(made, moves)]

    def group(refs, chip, core, here):
        blocks = [here] + [step(here, core) for step in steps]
        return [[((), EVERY, local(*refs[:2], chip, z) + [(ref, (z,)) for ref in refs[2:]])] for z in blocks]

    shapes = [f32(depth, width)] + [bf16(depth, width)] * len(steps)
    kept, *sends = sums([mine, core_in, *got], shapes, group, "group_sum")
    return [(kept, ())] + [(to_group(x, step, inner, outer), ()) for x, step in zip(sends, steps)]


CHIP_STEPS = [lambda chip, core: chip ^ (1 + core), lambda chip, core: chip ^ (2 - core)]
SPAN_STEPS, EARLY_STEPS = [[lambda z, core: z ^ 1, lambda z, core, far=far: z ^ far] for far in (2, 3)]
PARTNERS = [2, 3, 1]


def group_pieces(parts, refs, chip, z, index, more=()):
    out, at = [], 0
    for k, (mine, *_) in enumerate(parts):
        mine_ref, core_ref, got, last = refs[4 * k : 4 * k + 4]
        columns = pl.ds(at, mine.shape[-1])
        at += mine.shape[-1]
        terms = local(mine_ref, core_ref, chip, z) + [(got, (0, z)), (last, (z,))]
        out.append((index, columns, terms + [(ref.at[..., columns], lead) for ref, lead in more]))
    return out


def four_by_four(grads, width, inner, outer):
    chips = inner // CORES
    depth = grads.shape[1]
    widths = [width // 4] * 4
    wide = widths[0] + widths[1]
    order, last = [], {}
    parts = [[None, None] for _ in widths]

    def run(arrays, shapes, plan, name):
        made = sums(arrays, shapes, plan, name, order[-1:])
        order.append(made[0])
        return made

    def chip_targets(chip, core):
        return list(enumerate([CHIP_STEPS[0](chip, core), chip ^ 3]))

    def outer_targets(steps, here, core):
        return list(enumerate([steps[0](here, core), steps[1](steps[0](here, core), core)]))

    def over_chips(k):
        def plan(refs, chip, core, here):
            return [[((i, z), EVERY, local(*refs, to, z)) for i, to in chip_targets(chip, core) for z in range(outer)]]

        [made] = run(parts[k], [bf16(2, outer, depth, widths[k])], plan, "first_sum")
        parts[k].append(to_chip(made, CHIP_STEPS[0], chips))

    def over_chips_again(k):
        def plan(refs, chip, core, here):
            to = CHIP_STEPS[1](chip, core)
            return [[((z,), EVERY, local(*refs[:2], to, z) + [(refs[2], (1, z))]) for z in range(outer)]]

        [made] = run(parts[k], [bf16(outer, depth, widths[k])], plan, "second_sum")
        parts[k].append(to_chip(made, CHIP_STEPS[1], chips))

    def halve():
        def plan(refs, chip, core, here):
            return [[p for i, to in outer_targets(SPAN_STEPS, here, core) for p in group_pieces(parts[:2], refs, chip, to, (i,))]]

        [made] = run([*parts[0], *parts[1]], [bf16(2, depth, wide)], plan, "halve")
        last["halve"] = to_group(made, SPAN_STEPS[0], inner, outer)

    def halve_again():
        def plan(refs, chip, core, here):
            to = SPAN_STEPS[1](here, core)
            return [
                group_pieces(parts[:2], refs, chip, here, (), [(refs[-1], (0,))]),
                group_pieces(parts[:2], refs, chip, to, (), [(refs[-1], (1,))]),
            ]

        shapes = [f32(depth, wide), bf16(depth, wide)]
        kept, made = run([*parts[0], *parts[1], last["halve"]], shapes, plan, "halve_again")
        last["first"] = [(kept, ()), (to_group(made, SPAN_STEPS[1], inner, outer), ())]

    def group():
        def plan(refs, chip, core, here):
            return [group_pieces(parts[2:3], refs, chip, here ^ m, ()) for m in [0] + PARTNERS]

        shapes = [f32(depth, widths[2])] + [bf16(depth, widths[2])] * len(PARTNERS)
        kept, *sends = run(parts[2], shapes, plan, "group_sum")
        last["second"] = [(kept, ())]
        for x, m in zip(sends, PARTNERS):
            last["second"].append((to_group(x, lambda z, _, m=m: z ^ m, inner, outer), ()))

    def early():
        def plan(refs, chip, core, here):
            return [
                [((i, c), EVERY, local(*refs, c, to)) for i, to in outer_targets(EARLY_STEPS, here, core) for c in range(chips)]
            ]

        [made] = run(parts[3], [bf16(2, chips, depth, widths[3])], plan, "early_first")
        parts[3].append(to_group(made, EARLY_STEPS[0], inner, outer))

    def early_again():
        def plan(refs, chip, core, here):
            to = EARLY_STEPS[1](here, core)
            return [[((c,), EVERY, local(*refs[:2], c, to) + [(refs[2], (1, c))]) for c in range(chips)]]

        [made] = run(parts[3], [bf16(chips, depth, widths[3])], plan, "early_second")
        parts[3].append(to_group(made, EARLY_STEPS[1], inner, outer))

    def line(refs, c, here):
        return local(*refs[:2], c, here) + [(refs[2], (0, c)), (refs[3], (c,))]

    def early_chips():
        def plan(refs, chip, core, here):
            return [
                [((), EVERY, line(refs, chip, here))],
                [((i,), EVERY, line(refs, to, here)) for i, to in chip_targets(chip, core)],
            ]

        kept, made = run(parts[3], [f32(depth, widths[3]), bf16(2, depth, widths[3])], plan, "early_third")
        parts[3].append(to_chip(made, CHIP_STEPS[0], chips))
        last["third"] = [(kept, ()), (parts[3][4], (0,))]

    def early_chips_again():
        def plan(refs, chip, core, here):
            return [[((), EVERY, line(refs, CHIP_STEPS[1](chip, core), here) + [(refs[4], (1,))])]]

        [made] = run(parts[3], [bf16(depth, widths[3])], plan, "early_fourth")
        last["third"].append((to_chip(made, CHIP_STEPS[1], chips), ()))

    def theirs(k):
        place, grant = (sum(widths[:k]), widths[k]), 4 if order else 52
        order.append(load(grads, place, 1, width, chips, "load_theirs", order[-1:], grant))
        parts[k][1] = to_core(order[-1], inner)

    def ours(k):
        place = sum(widths[:k]), widths[k]
        order.append(load(grads, place, 0, width, chips, "load_mine", order[-1:]))
        parts[k][0] = order[-1]

    for k in (0, 3, 1, 2):
        theirs(k)
    ours(0)
    over_chips(0)
    ours(3)
    early()
    ours(1)
    over_chips(1)
    ours(2)
    over_chips(2)
    over_chips_again(0)
    over_chips_again(1)
    early_again()
    over_chips_again(2)
    halve()
    early_chips()
    group()
    halve_again()
    early_chips_again()
    return [[(wide, last["first"])], [(widths[2], last["second"]), (widths[3], last["third"])]]


def gather(own, inner, outer, straight):
    if outer == 4:
        if straight:
            pieces = {m: to_group(own, lambda z, _, m=m: z ^ m, inner, outer) for m in (2, 3, 1)}
        else:
            pieces = {m: to_group(own, lambda z, _, m=m: z ^ m, inner, outer) for m in (2, 1)}
            pieces[3] = to_group(pieces[2], lambda z, _: z ^ 1, inner, outer)
        return own, *[pieces[m] for m in (2, 1, 3)]
    return own, *[to_group(own, lambda z, _, s=s: (z + s) % outer, inner, outer) for s in range(1, outer)]


def body(gradients, master, first, second, *, inner, outer):
    depth, columns = gradients.shape[2:]
    chips, owned, width = inner // CORES, depth // outer, columns // inner
    grads = gradients.reshape(outer, owned, columns)
    state = (master, first, second)

    if chips == 4 and outer == 4 and width % (4 * LANES) == 0:
        totals = four_by_four(grads, width, inner, outer)
        sources = [lambda z, m=m: z ^ m for m in (0, 2, 1, 3)]
    else:
        sources = [lambda z, s=s: (z + outer - s) % outer for s in range(outer)]
        theirs, mine = [load(grads, (0, width), side, width, chips, "load") for side in (1, 0)]
        totals = [[(width, plain_total(mine, to_core(theirs, inner), inner, outer))]]

    sizes = [sum(size for size, _ in total) for total in totals]
    spans = [(sum(sizes[:k]), size) for k, size in enumerate(sizes)]
    made = [weights(total, span, state, "weights") for total, span in zip(totals, spans)]
    copy = assemble([gather(new, inner, outer, k == 0) for k, new in enumerate(made)], sources, spans, outer, width)
    return (*finish(totals, state), copy.reshape(depth, width))


def solution(mesh):
    return jax.shard_map(
        functools.partial(body, inner=mesh.shape["inner"], outer=mesh.shape["outer"]),
        mesh=mesh,
        in_specs=(
            P("inner", "outer", None, None),
            P("outer", "inner"),
            P("outer", "inner"),
            P("outer", "inner"),
        ),
        out_specs=(P("outer", "inner"), P("outer", "inner"), P("outer", "inner"), P(None, "inner")),
        check_vma=False,
    )
```

```python
import functools

import jax
import jax.numpy as jnp
from jax import lax
from jax.experimental import pallas as pl
from jax.experimental.pallas import tpu as pltpu
from jax.sharding import PartitionSpec as P

beta_first = 0.9
beta_second = 0.95
learn_rate = 0.05
decay_rate = 0.1
adam_eps = 1e-05
bias_first = 1.0 - 0.9**10
bias_second = 1.0 - 0.95**10

CORES = 2
STEP = 16
LANES = 128
ANY = pl.BlockSpec(memory_space=pl.ANY)
VMEM = pl.BlockSpec(memory_space=pltpu.VMEM)


def local_kernel(kernel, out_shape, operands, name, in_specs=None, out_specs=None, sems=0, after=(), grant=4):
    if in_specs is None:
        in_specs = [VMEM] * len(operands)
    if out_specs is None:
        out_specs = jax.tree.map(lambda _: VMEM, out_shape)
    n = len(operands)

    def ordered(*refs):
        kernel(*refs[:n], *refs[n + len(after) :])

    nbytes = sum(s.size * s.dtype.itemsize for s in jax.tree.leaves(out_shape)) * 3
    return pl.pallas_call(
        ordered,
        out_shape=out_shape,
        in_specs=in_specs + [ANY] * len(after),
        out_specs=out_specs,
        scratch_shapes=[pltpu.SemaphoreType.DMA((sems,))] if sems else [],
        compiler_params=pltpu.CompilerParams(vmem_limit_bytes=grant << 20),
        cost_estimate=pl.CostEstimate(flops=nbytes, bytes_accessed=nbytes, transcendentals=0),
        name=name,
    )(*operands, *after)


def bf16(*shape):
    return jax.ShapeDtypeStruct(shape, jnp.bfloat16)


def f32(*shape):
    return jax.ShapeDtypeStruct(shape, jnp.float32)


def place():
    me = lax.axis_index("inner")
    return me // CORES, lax.rem(me, CORES), lax.axis_index("outer")


def transfer(sources, targets, sems):
    copies = [pltpu.make_async_copy(s, d, sems.at[i]) for i, (s, d) in enumerate(zip(sources, targets))]
    for copy in copies:
        copy.start()
    for copy in copies:
        copy.wait()


def load(grads, span, side, width, chips, name, after=(), grant=4):
    outer, owned, _ = grads.shape
    base, size = span

    def kernel(grad_ref, out, sems):
        core = place()[1]
        sources = []
        for chip in range(chips):
            block = CORES * chip + (1 - core if side else core)
            sources.append(grad_ref.at[:, :, pl.ds(pl.multiple_of(block * width + base, LANES), size)])
        transfer(sources, [out.at[chip] for chip in range(chips)], sems)

    shape = bf16(chips, outer, owned, size)
    return local_kernel(kernel, shape, [grads], name, in_specs=[ANY], sems=chips, after=after, grant=grant)


def rows_at(start):
    return pl.ds(pl.multiple_of(start, STEP), STEP)


def each_step(depth, do):
    lax.fori_loop(0, depth // STEP, lambda i, carry: (do(rows_at(i * STEP)), carry)[1], 0, unroll=True)


def sum_of(terms, rows):
    value = None
    for ref, index in terms:
        term = ref[(*index, rows)].astype(jnp.float32)
        value = term if value is None else value + term
    return value


def sums(operands, shapes, plan, name, after=()):
    arrays = [x.grads if isinstance(x, Own) else x for x in operands]

    def kernel(*refs):
        outs = refs[len(operands) :]
        given = [x.with_ref(ref) if isinstance(x, Own) else ref for x, ref in zip(operands, refs)]
        for out, pieces in zip(outs, plan(given, *place())):
            for index, columns, terms in pieces:

                def do(rows, out=out, index=index, columns=columns, terms=terms):
                    out[(*index, rows, columns)] = sum_of(terms, rows).astype(out.dtype)

                each_step(out.shape[-2], do)

    return local_kernel(kernel, shapes, arrays, name, after=after)


def adam(total, master, first, second):
    new_first = beta_first * first + (1.0 - beta_first) * total
    new_second = beta_second * second + (1.0 - beta_second) * total * total
    update = new_first / bias_first / (jnp.sqrt(new_second / bias_second) + adam_eps) + decay_rate * master
    return master - learn_rate * update, new_first, new_second


def each_piece(total, refs, base=0):
    refs = list(refs)
    for size, terms in total:
        yield pl.ds(base, size), [(refs.pop(0), index) for _, index in terms]
        base += size


def arrays_of(total):
    return [array for _, terms in total for array, _ in terms]


def weights(total, span, state, name, after=()):
    arrays = arrays_of(total)
    depth = state[0].shape[0]

    def kernel(*refs):
        state_refs, out = refs[len(arrays) : -1], refs[-1]
        for columns, terms in each_piece(total, refs, span[0]):
            here = pl.ds(columns.start - span[0], columns.size)

            def do(rows, terms=terms, columns=columns, here=here):
                value, _, _ = adam(sum_of(terms, rows), *[ref[rows, columns] for ref in state_refs])
                out[rows, here] = value.astype(out.dtype)

            each_step(depth, do)

    return local_kernel(kernel, bf16(depth, span[1]), [*arrays, *state], name, after=after)


def finish(totals, state):
    total = [piece for pieces in totals for piece in pieces]
    arrays = arrays_of(total)
    n = len(arrays)

    def kernel(*refs):
        state_refs, outs = refs[n : n + 3], refs[n + 3 :]
        for columns, terms in each_piece(total, refs):

            def do(rows, terms=terms, columns=columns):
                values = adam(sum_of(terms, rows), *[ref[rows, columns] for ref in state_refs])
                for out, value in zip(outs, values):
                    out[rows, columns] = value

            each_step(state[0].shape[0], do)

    return local_kernel(kernel, [f32(*state[0].shape)] * 3, arrays + list(state), "finish")


def assemble(groups, sources, spans, outer, width):
    def kernel(*refs):
        *pieces, out, sems = refs
        here = lax.axis_index("outer")
        targets = [out.at[source(here), :, pl.ds(*span)] for span in spans for source in sources]
        transfer(pieces, targets, sems)

    operands = [piece for group in groups for piece in group]
    shape = bf16(outer, operands[0].shape[0], width)
    return local_kernel(kernel, shape, operands, "assemble", out_specs=ANY, sems=len(operands))


def to_core(x, inner):
    return lax.ppermute(x, "inner", [(i, i ^ 1) for i in range(inner)])


def to_chip(x, target, chips):
    pairs = [(CORES * c + k, CORES * target(c, k) + k) for c in range(chips) for k in range(CORES)]
    return lax.ppermute(x, "inner", pairs)


def to_group(x, target, inner, outer):
    pairs = [(i * outer + z, i * outer + target(z, i % CORES)) for i in range(inner) for z in range(outer)]
    return lax.ppermute(x, ("inner", "outer"), pairs)


class Own:
    def __init__(self, grads, base, size, width):
        self.grads, self.base, self.size, self.width = grads, base, size, width

    def with_ref(self, ref):
        return Own(ref, self.base, self.size, self.width)

    def term(self, chip, block):
        start = (CORES * chip + place()[1]) * self.width + self.base
        return self.grads.at[:, :, pl.ds(pl.multiple_of(start, LANES), self.size)], (block,)


def local(mine, core_in, chip, block):
    own = mine.term(chip, block) if isinstance(mine, Own) else (mine, (chip, block))
    return [own, (core_in, (chip, block))]


EVERY = slice(None)


def plain_total(mine, core_in, inner, outer):
    chips, _, depth, width = mine.shape
    moves = [lambda chip, core, m=m: (chip + m) % chips for m in range(1, chips)]
    steps = [lambda z, core, s=s: (z + s) % outer for s in range(1, outer)]

    def first(refs, chip, core, here):
        return [[((z,), EVERY, local(*refs, move(chip, core), z)) for z in range(outer)] for move in moves]

    made = sums([mine, core_in], [bf16(outer, depth, width)] * len(moves), first, "first_sum")
    got = [to_chip(x, move, chips) for x, move in zip(made, moves)]

    def group(refs, chip, core, here):
        blocks = [here] + [step(here, core) for step in steps]
        return [[((), EVERY, local(*refs[:2], chip, z) + [(ref, (z,)) for ref in refs[2:]])] for z in blocks]

    shapes = [f32(depth, width)] + [bf16(depth, width)] * len(steps)
    kept, *sends = sums([mine, core_in, *got], shapes, group, "group_sum")
    return [(kept, ())] + [(to_group(x, step, inner, outer), ()) for x, step in zip(sends, steps)]


CHIP_STEPS = [lambda chip, core: chip ^ (1 + core), lambda chip, core: chip ^ (2 - core)]
SPAN_STEPS, EARLY_STEPS = [[lambda z, core: z ^ 1, lambda z, core, far=far: z ^ far] for far in (2, 3)]
PARTNERS = [2, 3, 1]


def group_pieces(parts, refs, chip, z, index, more=()):
    out, at = [], 0
    for k, (_, core_in, *_) in enumerate(parts):
        mine_ref, core_ref, got, last = refs[4 * k : 4 * k + 4]
        columns = pl.ds(at, core_in.shape[-1])
        at += core_in.shape[-1]
        terms = local(mine_ref, core_ref, chip, z) + [(got, (0, z)), (last, (z,))]
        out.append((index, columns, terms + [(ref.at[..., columns], lead) for ref, lead in more]))
    return out


def four_by_four(grads, width, inner, outer):
    chips = inner // CORES
    depth = grads.shape[1]
    widths = [width // 4] * 4
    wide = widths[0] + widths[1]
    order, last = [], {}
    parts = [[Own(grads, sum(widths[:k]), size, width), None] for k, size in enumerate(widths)]

    def run(arrays, shapes, plan, name):
        made = sums(arrays, shapes, plan, name, order[-1:])
        order.append(made[0])
        return made

    def chip_targets(chip, core):
        return list(enumerate([CHIP_STEPS[0](chip, core), chip ^ 3]))

    def outer_targets(steps, here, core):
        return list(enumerate([steps[0](here, core), steps[1](steps[0](here, core), core)]))

    def over_chips(k):
        def plan(refs, chip, core, here):
            return [[((i, z), EVERY, local(*refs, to, z)) for i, to in chip_targets(chip, core) for z in range(outer)]]

        [made] = run(parts[k], [bf16(2, outer, depth, widths[k])], plan, "first_sum")
        parts[k].append(to_chip(made, CHIP_STEPS[0], chips))

    def over_chips_again(k):
        def plan(refs, chip, core, here):
            to = CHIP_STEPS[1](chip, core)
            return [[((z,), EVERY, local(*refs[:2], to, z) + [(refs[2], (1, z))]) for z in range(outer)]]

        [made] = run(parts[k], [bf16(outer, depth, widths[k])], plan, "second_sum")
        parts[k].append(to_chip(made, CHIP_STEPS[1], chips))

    def halve():
        def plan(refs, chip, core, here):
            return [[p for i, to in outer_targets(SPAN_STEPS, here, core) for p in group_pieces(parts[:2], refs, chip, to, (i,))]]

        [made] = run([*parts[0], *parts[1]], [bf16(2, depth, wide)], plan, "halve")
        last["halve"] = to_group(made, SPAN_STEPS[0], inner, outer)

    def halve_again():
        def plan(refs, chip, core, here):
            to = SPAN_STEPS[1](here, core)
            return [
                group_pieces(parts[:2], refs, chip, here, (), [(refs[-1], (0,))]),
                group_pieces(parts[:2], refs, chip, to, (), [(refs[-1], (1,))]),
            ]

        shapes = [f32(depth, wide), bf16(depth, wide)]
        kept, made = run([*parts[0], *parts[1], last["halve"]], shapes, plan, "halve_again")
        last["first"] = [(kept, ()), (to_group(made, SPAN_STEPS[1], inner, outer), ())]

    def group():
        def plan(refs, chip, core, here):
            return [group_pieces(parts[2:3], refs, chip, here ^ m, ()) for m in [0] + PARTNERS]

        shapes = [f32(depth, widths[2])] + [bf16(depth, widths[2])] * len(PARTNERS)
        kept, *sends = run(parts[2], shapes, plan, "group_sum")
        last["second"] = [(kept, ())]
        for x, m in zip(sends, PARTNERS):
            last["second"].append((to_group(x, lambda z, _, m=m: z ^ m, inner, outer), ()))

    def early():
        def plan(refs, chip, core, here):
            return [
                [((i, c), EVERY, local(*refs, c, to)) for i, to in outer_targets(EARLY_STEPS, here, core) for c in range(chips)]
            ]

        [made] = run(parts[3], [bf16(2, chips, depth, widths[3])], plan, "early_first")
        parts[3].append(to_group(made, EARLY_STEPS[0], inner, outer))

    def early_again():
        def plan(refs, chip, core, here):
            to = EARLY_STEPS[1](here, core)
            return [[((c,), EVERY, local(*refs[:2], c, to) + [(refs[2], (1, c))]) for c in range(chips)]]

        [made] = run(parts[3], [bf16(chips, depth, widths[3])], plan, "early_second")
        parts[3].append(to_group(made, EARLY_STEPS[1], inner, outer))

    def line(refs, c, here):
        return local(*refs[:2], c, here) + [(refs[2], (0, c)), (refs[3], (c,))]

    def early_chips():
        def plan(refs, chip, core, here):
            return [
                [((), EVERY, line(refs, chip, here))],
                [((i,), EVERY, line(refs, to, here)) for i, to in chip_targets(chip, core)],
            ]

        kept, made = run(parts[3], [f32(depth, widths[3]), bf16(2, depth, widths[3])], plan, "early_third")
        parts[3].append(to_chip(made, CHIP_STEPS[0], chips))
        last["third"] = [(kept, ()), (parts[3][4], (0,))]

    def early_chips_again():
        def plan(refs, chip, core, here):
            return [[((), EVERY, line(refs, CHIP_STEPS[1](chip, core), here) + [(refs[4], (1,))])]]

        [made] = run(parts[3], [bf16(depth, widths[3])], plan, "early_fourth")
        last["third"].append((to_chip(made, CHIP_STEPS[1], chips), ()))

    def theirs(k):
        place, grant = (sum(widths[:k]), widths[k]), 4 if order else 52
        order.append(load(grads, place, 1, width, chips, "load_theirs", order[-1:], grant))
        parts[k][1] = to_core(order[-1], inner)

    theirs(0)
    theirs(1)
    theirs(3)
    theirs(2)
    over_chips(0)
    early()
    over_chips(1)
    over_chips_again(0)
    over_chips(2)
    over_chips_again(1)
    early_again()
    over_chips_again(2)
    halve()
    early_chips()
    group()
    halve_again()
    early_chips_again()
    return [[(wide, last["first"])], [(widths[2], last["second"]), (widths[3], last["third"])]]


def gather(own, inner, outer, straight):
    if outer == 4:
        if straight:
            pieces = {m: to_group(own, lambda z, _, m=m: z ^ m, inner, outer) for m in (2, 3, 1)}
        else:
            pieces = {m: to_group(own, lambda z, _, m=m: z ^ m, inner, outer) for m in (2, 1)}
            pieces[3] = to_group(pieces[2], lambda z, _: z ^ 1, inner, outer)
        return own, *[pieces[m] for m in (2, 1, 3)]
    return own, *[to_group(own, lambda z, _, s=s: (z + s) % outer, inner, outer) for s in range(1, outer)]


def body(gradients, master, first, second, *, inner, outer):
    depth, columns = gradients.shape[2:]
    chips, owned, width = inner // CORES, depth // outer, columns // inner
    grads = gradients.reshape(outer, owned, columns)
    state = (master, first, second)

    if chips == 4 and outer == 4 and width % (4 * LANES) == 0:
        totals = four_by_four(grads, width, inner, outer)
        sources = [lambda z, m=m: z ^ m for m in (0, 2, 1, 3)]
    else:
        sources = [lambda z, s=s: (z + outer - s) % outer for s in range(outer)]
        theirs, mine = [load(grads, (0, width), side, width, chips, "load") for side in (1, 0)]
        totals = [[(width, plain_total(mine, to_core(theirs, inner), inner, outer))]]

    sizes = [sum(size for size, _ in total) for total in totals]
    spans = [(sum(sizes[:k]), size) for k, size in enumerate(sizes)]
    made = [weights(total, span, state, "weights") for total, span in zip(totals, spans)]
    copy = assemble([gather(new, inner, outer, k == 0) for k, new in enumerate(made)], sources, spans, outer, width)
    return (*finish(totals, state), copy.reshape(depth, width))


def solution(mesh):
    return jax.shard_map(
        functools.partial(body, inner=mesh.shape["inner"], outer=mesh.shape["outer"]),
        mesh=mesh,
        in_specs=(
            P("inner", "outer", None, None),
            P("outer", "inner"),
            P("outer", "inner"),
            P("outer", "inner"),
        ),
        out_specs=(P("outer", "inner"), P("outer", "inner"), P("outer", "inner"), P(None, "inner")),
        check_vma=False,
    )
```

```python
import functools

import jax
import jax.numpy as jnp
from jax import lax
from jax.experimental import pallas as pl
from jax.experimental.pallas import tpu as pltpu
from jax.sharding import PartitionSpec as P

beta_first = 0.9
beta_second = 0.95
learn_rate = 0.05
decay_rate = 0.1
adam_eps = 1e-05
bias_first = 1.0 - 0.9**10
bias_second = 1.0 - 0.95**10

CORES = 2
STEP = 16
LANES = 128
ANY = pl.BlockSpec(memory_space=pl.ANY)
VMEM = pl.BlockSpec(memory_space=pltpu.VMEM)


def local_kernel(kernel, out_shape, operands, name, in_specs=None, out_specs=None, sems=0, after=(), grant=4):
    if in_specs is None:
        in_specs = [VMEM] * len(operands)
    if out_specs is None:
        out_specs = jax.tree.map(lambda _: VMEM, out_shape)
    n = len(operands)

    def ordered(*refs):
        kernel(*refs[:n], *refs[n + len(after) :])

    nbytes = sum(s.size * s.dtype.itemsize for s in jax.tree.leaves(out_shape)) * 3
    return pl.pallas_call(
        ordered,
        out_shape=out_shape,
        in_specs=in_specs + [ANY] * len(after),
        out_specs=out_specs,
        scratch_shapes=[pltpu.SemaphoreType.DMA((sems,))] if sems else [],
        compiler_params=pltpu.CompilerParams(vmem_limit_bytes=grant << 20),
        cost_estimate=pl.CostEstimate(flops=nbytes, bytes_accessed=nbytes, transcendentals=0),
        name=name,
    )(*operands, *after)


def bf16(*shape):
    return jax.ShapeDtypeStruct(shape, jnp.bfloat16)


def f32(*shape):
    return jax.ShapeDtypeStruct(shape, jnp.float32)


def place():
    me = lax.axis_index("inner")
    return me // CORES, lax.rem(me, CORES), lax.axis_index("outer")


def transfer(sources, targets, sems):
    copies = [pltpu.make_async_copy(s, d, sems.at[i]) for i, (s, d) in enumerate(zip(sources, targets))]
    for copy in copies:
        copy.start()
    for copy in copies:
        copy.wait()


def load(grads, span, side, width, chips, name, after=(), grant=4):
    outer, owned, _ = grads.shape
    base, size = span

    def kernel(grad_ref, out, sems):
        core = place()[1]
        sources = []
        for chip in range(chips):
            block = CORES * chip + (1 - core if side else core)
            sources.append(grad_ref.at[:, :, pl.ds(pl.multiple_of(block * width + base, LANES), size)])
        transfer(sources, [out.at[chip] for chip in range(chips)], sems)

    shape = bf16(chips, outer, owned, size)
    return local_kernel(kernel, shape, [grads], name, in_specs=[ANY], sems=chips, after=after, grant=grant)


def rows_at(start):
    return pl.ds(pl.multiple_of(start, STEP), STEP)


def each_step(depth, do):
    lax.fori_loop(0, depth // STEP, lambda i, carry: (do(rows_at(i * STEP)), carry)[1], 0, unroll=True)


def sum_of(terms, rows):
    value = None
    for ref, index in terms:
        term = ref[(*index, rows)].astype(jnp.float32)
        value = term if value is None else value + term
    return value


def sums(operands, shapes, plan, name, after=()):
    arrays = [x.grads if isinstance(x, Own) else x for x in operands]

    def kernel(*refs):
        outs = refs[len(operands) :]
        given = [x.with_ref(ref) if isinstance(x, Own) else ref for x, ref in zip(operands, refs)]
        for out, pieces in zip(outs, plan(given, *place())):
            for index, columns, terms in pieces:

                def do(rows, out=out, index=index, columns=columns, terms=terms):
                    out[(*index, rows, columns)] = sum_of(terms, rows).astype(out.dtype)

                each_step(out.shape[-2], do)

    return local_kernel(kernel, shapes, arrays, name, after=after)


def adam(total, master, first, second):
    new_first = beta_first * first + (1.0 - beta_first) * total
    new_second = beta_second * second + (1.0 - beta_second) * total * total
    update = new_first / bias_first / (jnp.sqrt(new_second / bias_second) + adam_eps) + decay_rate * master
    return master - learn_rate * update, new_first, new_second


def each_piece(total, refs, base=0):
    refs = list(refs)
    for size, terms in total:
        yield pl.ds(base, size), [(refs.pop(0), index) for _, index in terms]
        base += size


def arrays_of(total):
    return [array for _, terms in total for array, _ in terms]


def weights(total, span, state, name, after=()):
    arrays = arrays_of(total)
    depth = state[0].shape[0]

    def kernel(*refs):
        state_refs, out = refs[len(arrays) : -1], refs[-1]
        for columns, terms in each_piece(total, refs, span[0]):
            here = pl.ds(columns.start - span[0], columns.size)

            def do(rows, terms=terms, columns=columns, here=here):
                value, _, _ = adam(sum_of(terms, rows), *[ref[rows, columns] for ref in state_refs])
                out[rows, here] = value.astype(out.dtype)

            each_step(depth, do)

    return local_kernel(kernel, bf16(depth, span[1]), [*arrays, *state], name, after=after)


def finish(totals, state):
    total = [piece for pieces in totals for piece in pieces]
    arrays = arrays_of(total)
    n = len(arrays)

    def kernel(*refs):
        state_refs, outs = refs[n : n + 3], refs[n + 3 :]
        for columns, terms in each_piece(total, refs):

            def do(rows, terms=terms, columns=columns):
                values = adam(sum_of(terms, rows), *[ref[rows, columns] for ref in state_refs])
                for out, value in zip(outs, values):
                    out[rows, columns] = value

            each_step(state[0].shape[0], do)

    return local_kernel(kernel, [f32(*state[0].shape)] * 3, arrays + list(state), "finish")


def assemble(groups, sources, spans, outer, width):
    def kernel(*refs):
        *pieces, out, sems = refs
        here = lax.axis_index("outer")
        targets = [out.at[source(here), :, pl.ds(*span)] for span in spans for source in sources]
        transfer(pieces, targets, sems)

    operands = [piece for group in groups for piece in group]
    shape = bf16(outer, operands[0].shape[0], width)
    return local_kernel(kernel, shape, operands, "assemble", out_specs=ANY, sems=len(operands))


def to_core(x, inner):
    return lax.ppermute(x, "inner", [(i, i ^ 1) for i in range(inner)])


def to_chip(x, target, chips):
    pairs = [(CORES * c + k, CORES * target(c, k) + k) for c in range(chips) for k in range(CORES)]
    return lax.ppermute(x, "inner", pairs)


def to_group(x, target, inner, outer):
    pairs = [(i * outer + z, i * outer + target(z, i % CORES)) for i in range(inner) for z in range(outer)]
    return lax.ppermute(x, ("inner", "outer"), pairs)


class Own:
    def __init__(self, grads, base, size, width):
        self.grads, self.base, self.size, self.width = grads, base, size, width

    def with_ref(self, ref):
        return Own(ref, self.base, self.size, self.width)

    def term(self, chip, block):
        start = (CORES * chip + place()[1]) * self.width + self.base
        return self.grads.at[:, :, pl.ds(pl.multiple_of(start, LANES), self.size)], (block,)


def local(mine, core_in, chip, block):
    own = mine.term(chip, block) if isinstance(mine, Own) else (mine, (chip, block))
    return [own, (core_in, (chip, block))]


EVERY = slice(None)


def plain_total(mine, core_in, inner, outer):
    chips, _, depth, width = mine.shape
    moves = [lambda chip, core, m=m: (chip + m) % chips for m in range(1, chips)]
    steps = [lambda z, core, s=s: (z + s) % outer for s in range(1, outer)]

    def first(refs, chip, core, here):
        return [[((z,), EVERY, local(*refs, move(chip, core), z)) for z in range(outer)] for move in moves]

    made = sums([mine, core_in], [bf16(outer, depth, width)] * len(moves), first, "first_sum")
    got = [to_chip(x, move, chips) for x, move in zip(made, moves)]

    def group(refs, chip, core, here):
        blocks = [here] + [step(here, core) for step in steps]
        return [[((), EVERY, local(*refs[:2], chip, z) + [(ref, (z,)) for ref in refs[2:]])] for z in blocks]

    shapes = [f32(depth, width)] + [bf16(depth, width)] * len(steps)
    kept, *sends = sums([mine, core_in, *got], shapes, group, "group_sum")
    return [(kept, ())] + [(to_group(x, step, inner, outer), ()) for x, step in zip(sends, steps)]


CHIP_STEPS = [lambda chip, core: chip ^ (1 + core), lambda chip, core: chip ^ (2 - core)]
SPAN_STEPS, EARLY_STEPS = [[lambda z, core: z ^ 1, lambda z, core, far=far: z ^ far] for far in (2, 3)]
PARTNERS = [2, 3, 1]


def group_pieces(parts, refs, chip, z, index, more=()):
    out, at = [], 0
    for k, (_, core_in, *_) in enumerate(parts):
        mine_ref, core_ref, got, last = refs[4 * k : 4 * k + 4]
        columns = pl.ds(at, core_in.shape[-1])
        at += core_in.shape[-1]
        terms = local(mine_ref, core_ref, chip, z) + [(got, (0, z)), (last, (z,))]
        out.append((index, columns, terms + [(ref.at[..., columns], lead) for ref, lead in more]))
    return out


def four_by_four(grads, width, inner, outer):
    chips = inner // CORES
    depth = grads.shape[1]
    widths = [width // 4] * 4
    wide = widths[0] + widths[1]
    order, last = [], {}
    parts = [[Own(grads, sum(widths[:k]), size, width), None] for k, size in enumerate(widths)]

    def run(arrays, shapes, plan, name):
        made = sums(arrays, shapes, plan, name, order[-1:])
        order.append(made[0])
        return made

    def chip_targets(chip, core):
        return list(enumerate([CHIP_STEPS[0](chip, core), chip ^ 3]))

    def outer_targets(steps, here, core):
        return list(enumerate([steps[0](here, core), steps[1](steps[0](here, core), core)]))

    def over_chips(k):
        def plan(refs, chip, core, here):
            return [[((i, z), EVERY, local(*refs, to, z)) for i, to in chip_targets(chip, core) for z in range(outer)]]

        [made] = run(parts[k], [bf16(2, outer, depth, widths[k])], plan, "first_sum")
        parts[k].append(to_chip(made, CHIP_STEPS[0], chips))

    def over_chips_again(k):
        def plan(refs, chip, core, here):
            to = CHIP_STEPS[1](chip, core)
            return [[((z,), EVERY, local(*refs[:2], to, z) + [(refs[2], (1, z))]) for z in range(outer)]]

        [made] = run(parts[k], [bf16(outer, depth, widths[k])], plan, "second_sum")
        parts[k].append(to_chip(made, CHIP_STEPS[1], chips))

    def halve():
        def plan(refs, chip, core, here):
            return [[p for i, to in outer_targets(SPAN_STEPS, here, core) for p in group_pieces(parts[:2], refs, chip, to, (i,))]]

        [made] = run([*parts[0], *parts[1]], [bf16(2, depth, wide)], plan, "halve")
        last["halve"] = to_group(made, SPAN_STEPS[0], inner, outer)

    def halve_again():
        def plan(refs, chip, core, here):
            to = SPAN_STEPS[1](here, core)
            return [
                group_pieces(parts[:2], refs, chip, here, (), [(refs[-1], (0,))]),
                group_pieces(parts[:2], refs, chip, to, (), [(refs[-1], (1,))]),
            ]

        shapes = [f32(depth, wide), bf16(depth, wide)]
        kept, made = run([*parts[0], *parts[1], last["halve"]], shapes, plan, "halve_again")
        last["first"] = [(kept, ()), (to_group(made, SPAN_STEPS[1], inner, outer), ())]

    def group():
        def plan(refs, chip, core, here):
            return [group_pieces(parts[2:3], refs, chip, here ^ m, ()) for m in [0] + PARTNERS]

        shapes = [f32(depth, widths[2])] + [bf16(depth, widths[2])] * len(PARTNERS)
        kept, *sends = run(parts[2], shapes, plan, "group_sum")
        last["second"] = [(kept, ())]
        for x, m in zip(sends, PARTNERS):
            last["second"].append((to_group(x, lambda z, _, m=m: z ^ m, inner, outer), ()))

    def early():
        def plan(refs, chip, core, here):
            return [
                [((i, c), EVERY, local(*refs, c, to)) for i, to in outer_targets(EARLY_STEPS, here, core) for c in range(chips)]
            ]

        [made] = run(parts[3], [bf16(2, chips, depth, widths[3])], plan, "early_first")
        parts[3].append(to_group(made, EARLY_STEPS[0], inner, outer))

    def early_again():
        def plan(refs, chip, core, here):
            to = EARLY_STEPS[1](here, core)
            return [[((c,), EVERY, local(*refs[:2], c, to) + [(refs[2], (1, c))]) for c in range(chips)]]

        [made] = run(parts[3], [bf16(chips, depth, widths[3])], plan, "early_second")
        parts[3].append(to_group(made, EARLY_STEPS[1], inner, outer))

    def line(refs, c, here):
        return local(*refs[:2], c, here) + [(refs[2], (0, c)), (refs[3], (c,))]

    def early_chips():
        def plan(refs, chip, core, here):
            return [
                [((), EVERY, line(refs, chip, here))],
                [((i,), EVERY, line(refs, to, here)) for i, to in chip_targets(chip, core)],
            ]

        kept, made = run(parts[3], [f32(depth, widths[3]), bf16(2, depth, widths[3])], plan, "early_third")
        parts[3].append(to_chip(made, CHIP_STEPS[0], chips))
        last["third"] = [(kept, ()), (parts[3][4], (0,))]

    def early_chips_again():
        def plan(refs, chip, core, here):
            return [[((), EVERY, line(refs, CHIP_STEPS[1](chip, core), here) + [(refs[4], (1,))])]]

        [made] = run(parts[3], [bf16(depth, widths[3])], plan, "early_fourth")
        last["third"].append((to_chip(made, CHIP_STEPS[1], chips), ()))

    def theirs(k):
        place, grant = (sum(widths[:k]), widths[k]), 4 if order else 52
        order.append(load(grads, place, 1, width, chips, "load_theirs", order[-1:], grant))
        parts[k][1] = to_core(order[-1], inner)

    theirs(0)
    theirs(1)
    theirs(3)
    theirs(2)
    over_chips(0)
    early()
    over_chips(1)
    over_chips_again(0)
    over_chips(2)
    over_chips_again(1)
    early_again()
    over_chips_again(2)
    halve()
    early_chips()
    group()
    halve_again()
    early_chips_again()
    return [[(wide, last["first"])], [(widths[2], last["second"]), (widths[3], last["third"])]]


def gather(own, inner, outer, straight):
    if outer == 4:
        if straight:
            pieces = {m: to_group(own, lambda z, _, m=m: z ^ m, inner, outer) for m in (2, 3, 1)}
        else:
            pieces = {m: to_group(own, lambda z, _, m=m: z ^ m, inner, outer) for m in (2, 1)}
            pieces[3] = to_group(pieces[2], lambda z, _: z ^ 1, inner, outer)
        return own, *[pieces[m] for m in (2, 1, 3)]
    return own, *[to_group(own, lambda z, _, s=s: (z + s) % outer, inner, outer) for s in range(1, outer)]


def body(gradients, master, first, second, *, inner, outer):
    depth, columns = gradients.shape[2:]
    chips, owned, width = inner // CORES, depth // outer, columns // inner
    grads = gradients.reshape(outer, owned, columns)
    state = (master, first, second)

    if chips == 4 and outer == 4 and width % (4 * LANES) == 0:
        totals = four_by_four(grads, width, inner, outer)
        sources = [lambda z, m=m: z ^ m for m in (0, 2, 1, 3)]
    else:
        sources = [lambda z, s=s: (z + outer - s) % outer for s in range(outer)]
        theirs, mine = [load(grads, (0, width), side, width, chips, "load") for side in (1, 0)]
        totals = [[(width, plain_total(mine, to_core(theirs, inner), inner, outer))]]

    sizes = [sum(size for size, _ in total) for total in totals]
    spans = [(sum(sizes[:k]), size) for k, size in enumerate(sizes)]
    made = []
    for total, span in list(zip(totals, spans))[::-1]:
        made.insert(0, weights(total, span, state, "weights", made[:1]))
    copy = assemble([gather(new, inner, outer, k == 0) for k, new in enumerate(made)], sources, spans, outer, width)
    return (*finish(totals, state), copy.reshape(depth, width))


def solution(mesh):
    return jax.shard_map(
        functools.partial(body, inner=mesh.shape["inner"], outer=mesh.shape["outer"]),
        mesh=mesh,
        in_specs=(
            P("inner", "outer", None, None),
            P("outer", "inner"),
            P("outer", "inner"),
            P("outer", "inner"),
        ),
        out_specs=(P("outer", "inner"), P("outer", "inner"), P("outer", "inner"), P(None, "inner")),
        check_vma=False,
    )
```
